512 devices in a mesh: batch: 16 (over z), item: 32 (over x, y, core).
Axes of the slice: x: 4, y: 4, z: 16, core: 2. Of those that a mesh axis runs over, the one named last changes fastest.
Arguments:
- item_feat: bfloat16 [262144, 768], P(('batch', 'item')), may hold values from -6 to 6
- item_latent: bfloat16 [262144, 64], P(('batch', 'item')), may hold values from -1.5 to 1.5
- item_bias: bfloat16 [262144], P(('batch', 'item')), may hold values from -3 to 3
- projection: bfloat16 [768, 64], replicated, may hold values from -0.21875 to 0.21875
- user_factors: bfloat16 [131072, 128], P(('batch', 'item')), may hold values from -1.5 to 1.5
- user_ids: int32 [1048576], P(('batch', 'item')), may hold values from 0 to 255
- requests: int32 [16, 32, 32, 64], P('batch', 'item'), may hold values from 0 to 511, as said below
- pos_slot: int32 [1048576], P(('batch', 'item')), may hold values from 0 to 2047, as said below
- neg_slot: int32 [1048576], P(('batch', 'item')), may hold values from 0 to 2047, as said below
Outputs:
- item_latent_grad: float32 [262144, 64], P(('batch', 'item'))
- item_bias_grad: float32 [262144], P(('batch', 'item'))
- user_grad: float32 [131072, 128], P(('batch', 'item'))
- projection_grad: float32 [768, 64], replicated
The draws below stay inside these ranges and needn't reach their ends.
Inputs may be any that keep to these rules, and one draw needn't show every extreme that they name: `requests`: within one device and one owner the 64 rows are distinct. Every slot holds a row; the triples of a device name only some of its slots. `pos_slot`: names a slot of the triple's device; low slots and low owners are named far more often. `neg_slot`: names a slot of the triple's device.
All inputs are finite; a program needn't handle non-finite values.
Results may differ from the reference program's by a relative error of at most 0.008.
Values may be sent and summed in bfloat16 or wider, within the bound.
No kernel may reach another device: no remote copies, remote signals or barrier semaphores. Data moves between devices by JAX's collectives and lax.ppermute only.
A program may use at most 64 MiB of HBM per device.

```python
import math
import jax
import jax.numpy as jnp
from jax import lax

F = 768
K = 64
TRI_DEV = 2048
USERS_DEV = 256
ROWS_ITEM = 512
CAP = 64
TRIPLES = 1048576
USERS = 131072
ITEMS = 262144
N_BATCH = 16
N_ITEM = 32


def request_plan(key):
    devices = N_BATCH * N_ITEM
    key_shift, key_top, key_perm, key_first, key_second, key_other = jax.random.split(key, 6)
    shifts = jax.random.randint(key_shift, (devices, N_ITEM), 0, 4)
    counts = CAP // jnp.power(2, shifts)
    top = jax.random.randint(key_top, (devices,), 0, N_ITEM)
    owner_index = jnp.arange(N_ITEM)[None, :]
    full = (owner_index == top[:, None]) | (owner_index == N_ITEM - 1)
    counts = jnp.where(full, CAP, counts).astype(jnp.int32)
    perm_keys = jax.random.split(key_perm, devices * N_ITEM)
    rows = jax.vmap(lambda k: jax.random.permutation(k, ROWS_ITEM)[:CAP])(perm_keys)
    rows = rows.reshape(N_BATCH, N_ITEM, N_ITEM, CAP).astype(jnp.int32)
    live = jnp.sum(counts, 1)
    ends = jnp.cumsum(counts, 1)
    starts = ends - counts
    first = jax.random.randint(key_first, (devices, TRI_DEV), 0, live[:, None])
    second = jax.random.randint(key_second, (devices, TRI_DEV), 0, live[:, None])
    popular = first * second // live[:, None]
    other = jax.random.randint(key_other, (devices, TRI_DEV), 0, live[:, None])
    popular = popular.at[:, 0].set(0).at[:, 1].set(live - 1)
    other = other.at[:, 0].set(live - 1).at[:, 1].set(0)

    def locate(rank):
        owner = jnp.sum((ends[:, None, :] <= rank[:, :, None]).astype(jnp.int32), -1)
        offset = rank - jnp.take_along_axis(starts, owner, 1)
        return (owner * CAP + offset).reshape(-1).astype(jnp.int32)
    return (rows, locate(popular), locate(other))


def draw_requests(key, part):
    rows, positive, negative = request_plan(key)
    return rows


def draw_pos_slot(key, part):
    rows, positive, negative = request_plan(key)
    return positive


def draw_neg_slot(key, part):
    rows, positive, negative = request_plan(key)
    return negative


def plant(drawn, key, low, top_value):
    shape = drawn.shape
    place = [jax.random.randint(jax.random.fold_in(key, axis), (), 0, shape[axis]) for axis in range(len(shape))]
    drawn = drawn.at[tuple(place)].set(low)
    longest = shape.index(max(shape))
    place[longest] = (place[longest] + 1) % shape[longest]
    return drawn.at[tuple(place)].set(top_value)


def steps_of(rng, extent, cuts, least, top_value):
    def one(axis_at, blocks):
        steps = jax.random.uniform(jax.random.fold_in(jax.random.fold_in(rng, 6), axis_at), (blocks,), jnp.float32, least / len(cuts), top_value / len(cuts))
        return jnp.repeat(jnp.exp(steps), extent[axis_at] // blocks).reshape((-1,) + (1,) * (len(extent) - axis_at - 1))

    gain = one(*cuts[0])
    for cut in cuts[1:]:
        gain = gain * one(*cut)
    return gain


def scatter_about(stream_key, extent, deviation, limit, shards=(), kind=jnp.bfloat16):
    result = jax.random.normal(stream_key, extent, jnp.float32) * deviation
    if len(shards) > 0:
        result = steps_of(stream_key, extent, shards, -0.22, 0.18) * result
    return jnp.clip(result, min=-limit, max=limit).astype(kind)


def setup_inputs(seed: int = 0) -> dict:
    streams_of = jax.random.split(jax.random.key(seed), 10)
    item_feat = scatter_about(streams_of[0], (ITEMS, F), 1.0, 6.0, ((0, 512),))
    item_latent = scatter_about(streams_of[1], (ITEMS, K), 0.25, 1.5, ((0, 512),))
    item_bias = scatter_about(streams_of[2], (ITEMS,), 0.5, 3.0, ((0, 512),))
    projection = scatter_about(streams_of[3], (F, K), F ** -0.5, 0.21875)
    user_factors = scatter_about(streams_of[4], (USERS, 2 * K), 0.25, 1.5, ((0, 512),))
    user_ids = plant(jax.random.randint(streams_of[5], (TRIPLES,), 0, USERS_DEV), jax.random.fold_in(streams_of[5], 1), 0, USERS_DEV - 1).astype(jnp.int32)
    requests = draw_requests(jax.random.fold_in(streams_of[9], 71), 0)
    pos_slot = draw_pos_slot(jax.random.fold_in(streams_of[9], 71), 0)
    neg_slot = draw_neg_slot(jax.random.fold_in(streams_of[9], 71), 0)
    return {"item_feat": item_feat, "item_latent": item_latent, "item_bias": item_bias, "projection": projection, "user_factors": user_factors, "user_ids": user_ids, "requests": requests, "pos_slot": pos_slot, "neg_slot": neg_slot}


def reference(item_feat, item_latent, item_bias, projection, user_factors, user_ids, requests, pos_slot, neg_slot):
    slots = N_ITEM * CAP
    group_rows = N_ITEM * ROWS_ITEM
    feat_all = item_feat.reshape(N_BATCH, group_rows, F)
    lat_all = item_latent.reshape(N_BATCH, group_rows, K)
    bias_all = item_bias.reshape(N_BATCH, group_rows)
    users_all = user_factors.reshape(N_BATCH, N_ITEM, USERS_DEV, 2 * K)
    uid_all = user_ids.reshape(N_BATCH, N_ITEM, TRI_DEV)
    pos_all = pos_slot.reshape(N_BATCH, N_ITEM, TRI_DEV)
    neg_all = neg_slot.reshape(N_BATCH, N_ITEM, TRI_DEV)
    owner_base = (jnp.arange(N_ITEM, dtype=jnp.int32) * ROWS_ITEM)[None, :, None]
    flat_all = (requests + owner_base).reshape(N_BATCH, N_ITEM, slots).astype(jnp.int32)

    def group(inputs):
        feat, lat, bias, users, uids, poss, negs, flat = inputs
        visual = jnp.dot(feat, projection, preferred_element_type=jnp.float32).astype(jnp.bfloat16)

        def source(user_rows, uid, pos, neg, slot_rows):
            lat_s = jnp.take(lat, slot_rows, axis=0).astype(jnp.float32)
            vis_s = jnp.take(visual, slot_rows, axis=0).astype(jnp.float32)
            bias_s = jnp.take(bias, slot_rows, axis=0).astype(jnp.float32)
            urow = jnp.take(user_rows, uid, axis=0).astype(jnp.float32)
            dlat = jnp.take(lat_s, pos, axis=0) - jnp.take(lat_s, neg, axis=0)
            dvis = jnp.take(vis_s, pos, axis=0) - jnp.take(vis_s, neg, axis=0)
            score = lax.optimization_barrier(jnp.sum(urow[:, :K] * dlat, 1)) + lax.optimization_barrier(jnp.sum(urow[:, K:] * dvis, 1))
            score = score + jnp.take(bias_s, pos) - jnp.take(bias_s, neg)
            slope = -jax.nn.sigmoid(-score)
            ugrad = jax.ops.segment_sum(jnp.concatenate([slope[:, None] * dlat, slope[:, None] * dvis], 1), uid, num_segments=USERS_DEV)
            values = jnp.concatenate([slope[:, None] * urow, slope[:, None]], 1)
            slot_grad = jax.ops.segment_sum(jnp.concatenate([values, -values], 0), jnp.concatenate([pos, neg], 0), num_segments=slots)
            return (ugrad, slot_grad)
        ugrad, slot_grad = jax.vmap(source)(users, uids, poss, negs, flat)
        coef_b = lax.optimization_barrier(slot_grad[:, :, K:2 * K].astype(jnp.bfloat16))
        packed = jnp.concatenate([slot_grad[:, :, :K], coef_b.astype(jnp.float32), slot_grad[:, :, 2 * K:]], 2)
        row_sum = jax.ops.segment_sum(packed.reshape(N_ITEM * slots, 2 * K + 1), flat.reshape(-1), num_segments=group_rows)
        term = jnp.dot(feat.astype(jnp.float32).T, row_sum[:, K:2 * K], precision=lax.Precision.HIGHEST)
        return (ugrad, row_sum[:, :K], row_sum[:, 2 * K], term)
    ugrad, lat_grad, bias_grad, terms = lax.map(group, (feat_all, lat_all, bias_all, users_all, uid_all, pos_all, neg_all, flat_all))
    projection_grad = lax.optimization_barrier(jnp.sum(terms, 0)) / math.sqrt(TRIPLES)
    return (lat_grad.reshape(ITEMS, K), bias_grad.reshape(ITEMS), ugrad.reshape(USERS, 2 * K), projection_grad)
```

```python
import functools
import math

import jax
import jax.numpy as jnp
from jax import lax
from jax.experimental import pallas as pl
from jax.experimental.pallas import tpu as pltpu
from jax.sharding import PartitionSpec as P

BF = jnp.bfloat16
F32 = jnp.float32
VM = pl.BlockSpec(memory_space=pltpu.VMEM)
NN = (((1,), (0,)), ((), ()))
NT = (((1,), (1,)), ((), ()))
MIB = 1024 * 1024


def mm(a, b, dims=NN):
    return lax.dot_general(a, b, dims, preferred_element_type=F32)


def split(x):
    hi = x.astype(BF)
    return hi, (x - hi.astype(F32)).astype(BF)


def one_hot(rows, index):
    n = index.shape[1]
    return (lax.broadcasted_iota(jnp.int32, (rows, n), 0) == index).astype(F32)


def lane_index(ref, first, count):
    return jnp.concatenate([ref[r : r + 1, :] for r in range(first, first + count)], axis=1)


def pack(out_ref, owner, block, width, cap):
    lat, vis, bias = block[:width], block[width : 2 * width], block[2 * width : 2 * width + 8]
    out_ref[owner, 0:width, :] = jnp.concatenate([lat, vis], axis=1).astype(BF)
    out_ref[owner, width : width + 8, :] = jnp.concatenate(
        [bias, jnp.zeros((8, cap), F32)], axis=1
    ).astype(BF)


def unpack(in_ref, flat_ref, width, cap):
    owners = in_ref.shape[0]
    for o in range(0, owners, 2):
        a, b = in_ref[o].astype(F32), in_ref[o + 1].astype(F32)
        cols = slice(o * cap, (o + 2) * cap)
        lat = jnp.concatenate([a[:width, :cap], b[:width, :cap]], axis=1)
        vis = jnp.concatenate([a[:width, cap:], b[:width, cap:]], axis=1)
        bias = jnp.concatenate([a[width:, :cap], b[width:, :cap]], axis=1)
        flat_ref[0:width, cols] = lat.astype(BF)
        flat_ref[width : 2 * width, cols] = vis.astype(BF)
        flat_ref[2 * width :, cols] = jnp.concatenate(
            [bias, jnp.zeros((8, 2 * cap), F32)], axis=0
        ).astype(BF)


def table_kernel(feat_ref, lat_ref, bias_ref, proj_ref, out_ref):
    width, rows = lat_ref.shape
    out_ref[0:width, :] = lat_ref[...]
    out_ref[width : 2 * width, :] = mm(proj_ref[...], feat_ref[...], NT).astype(BF)
    first = lax.broadcasted_iota(jnp.int32, (16, rows), 0) == 0
    bias = jnp.where(first, bias_ref[...].astype(F32), 0.0)
    out_ref[2 * width :, :] = bias.astype(BF)


def send_kernel(table_ref, asked_ref, out_ref):
    owners, cap = asked_ref.shape
    rows = table_ref.shape[1]
    width = (table_ref.shape[0] - 16) // 2
    table = table_ref[...]
    for o in range(0, owners, 4):
        hot = one_hot(rows, lane_index(asked_ref, o, 4)).astype(BF)
        got = mm(table, hot)
        for k in range(4):
            pack(out_ref, o + k, got[:, k * cap : (k + 1) * cap], width, cap)


def user_kernel(user_ref, uid_ref, out_ref):
    users, width2 = user_ref.shape
    table = jnp.transpose(user_ref[...].astype(F32)).astype(BF)
    step = uid_ref.shape[1]
    for r in range(0, uid_ref.shape[0], 2):
        hot = one_hot(users, lane_index(uid_ref, r, 2)).astype(BF)
        out_ref[:, r * step : (r + 2) * step] = mm(table, hot).astype(BF)


def triple_kernel(
    got_ref, user_ref, pos_ref, neg_ref, uid_ref, send_ref, ugrad_ref, flat, diff, grad, ugd, *, users
):
    owners, cap = got_ref.shape[0], got_ref.shape[2] // 2
    width = got_ref.shape[1] - 8
    slots = owners * cap
    w2 = 2 * width
    unpack(got_ref, flat, width, cap)
    step = 2 * pos_ref.shape[1]
    table = flat[...]
    for r in range(0, pos_ref.shape[0], 2):
        cols = slice(r // 2 * step, (r // 2 + 1) * step)
        d = one_hot(slots, lane_index(pos_ref, r, 2)) - one_hot(slots, lane_index(neg_ref, r, 2))
        d = d.astype(BF)
        diff[:, cols] = d
        delta = mm(table, d)
        u = user_ref[:, cols].astype(F32)
        x = jnp.sum(u * delta[:w2], axis=0, keepdims=True) + delta[w2 : w2 + 1]
        g = -jax.nn.sigmoid(-x)
        hi, lo = split(g * u)
        first = lax.broadcasted_iota(jnp.int32, (16, step), 0) == 0
        bhi, blo = split(jnp.where(first, g, 0.0))
        grad[0:w2, cols] = hi
        grad[w2 : w2 + 16, cols] = bhi
        grad[w2 + 16 : 2 * w2 + 16, cols] = lo
        grad[2 * w2 + 16 :, cols] = blo
        hi, lo = split(g * delta[:w2])
        ugd[0:w2, cols] = hi
        ugd[w2:, cols] = lo
    coef = grad[...]
    for o in range(0, owners, 4):
        both = mm(coef, diff[o * cap : (o + 4) * cap, :], NT)
        total = both[: w2 + 16] + both[w2 + 16 :]
        for k in range(4):
            pack(send_ref, o + k, total[:, k * cap : (k + 1) * cap], width, cap)
    hot = one_hot(users, lane_index(uid_ref, 0, uid_ref.shape[0])).astype(BF)
    both = mm(hot, ugd[...], NT)
    ugrad_ref[...] = both[:, :w2] + both[:, w2:]


def row_kernel(back_ref, asked_ref, feat_ref, lat_ref, bias_ref, term_ref, flat):
    owners, cap = asked_ref.shape
    width = back_ref.shape[1] - 8
    rows, feats = feat_ref.shape
    unpack(back_ref, flat, width, cap)
    hot = one_hot(rows, lane_index(asked_ref, 0, owners)).astype(BF)
    total = mm(flat[...], hot, NT)
    lat_ref[...] = total[:width]
    bias_ref[...] = total[2 * width : 2 * width + 1]
    hi, lo = split(total[width : 2 * width])
    both = mm(jnp.concatenate([hi, lo], axis=0), feat_ref[...])
    term = both[:width] + both[width:]
    across = feats // 128
    tiles = [(i, j) for i in range(width // 8) for j in range(across)]
    per = term_ref.shape[1] // 8
    for t in range(owners * per):
        o, k = divmod(t, per)
        if t < len(tiles):
            i, j = tiles[t]
            tile = term[8 * i : 8 * i + 8, 128 * j : 128 * j + 128]
        else:
            tile = jnp.zeros((8, 128), F32)
        term_ref[o, 8 * k : 8 * k + 8, :] = tile


def sum_kernel(in_ref, out_ref, *, scale):
    total = in_ref[0]
    for k in range(1, in_ref.shape[0]):
        total = total + in_ref[k]
    out_ref[...] = jnp.broadcast_to((total * scale)[None], out_ref.shape)


def join_kernel(in_ref, out_ref):
    across = out_ref.shape[1] // 128
    per = in_ref.shape[1] // 8
    for t in range(out_ref.shape[0] // 8 * across):
        i, j = divmod(t, across)
        o, k = divmod(t, per)
        out_ref[8 * i : 8 * i + 8, 128 * j : 128 * j + 128] = in_ref[o, 8 * k : 8 * k + 8, :]


def call(kernel, out, *args, scratch=(), limit=32, flops=0, moved=0):
    many = isinstance(out, (list, tuple))
    return pl.pallas_call(
        kernel,
        out_shape=out,
        in_specs=[VM] * len(args),
        out_specs=[VM] * len(out) if many else VM,
        scratch_shapes=list(scratch),
        compiler_params=pltpu.CompilerParams(vmem_limit_bytes=limit * MIB),
        cost_estimate=pl.CostEstimate(flops=flops, bytes_accessed=moved, transcendentals=0),
    )(*args)


def shape(dims, dtype):
    return jax.ShapeDtypeStruct(dims, dtype)


def exchange(x, axis):
    return lax.all_to_all(x, axis, split_axis=0, concat_axis=0, tiled=True)


def on_device(
    item_feat,
    item_latent,
    item_bias,
    projection,
    user_factors,
    user_ids,
    requests,
    pos_slot,
    neg_slot,
):
    owners = lax.axis_size("item")
    groups = lax.axis_size("batch")
    rows, feats = item_feat.shape
    width = item_latent.shape[1]
    users = user_factors.shape[0]
    cap = requests.shape[-1]
    slots = owners * cap
    triples = pos_slot.shape[0]
    w2 = 2 * width
    high = w2 + 16
    lines = triples // 128

    asked = exchange(requests.reshape(owners, cap), "item")
    table = call(
        table_kernel,
        shape((high, rows), BF),
        item_feat,
        item_latent.T,
        item_bias.reshape(1, rows),
        projection.T,
        flops=2 * rows * feats * width,
        moved=2 * rows * (feats + high),
    )
    pos = pos_slot.reshape(lines, 128)
    neg = neg_slot.reshape(lines, 128)
    uid = user_ids.reshape(lines, 128)
    user_rows = call(
        user_kernel,
        shape((w2, triples), BF),
        user_factors,
        uid,
        flops=2 * users * w2 * triples,
        moved=4 * w2 * triples,
    )
    message = shape((owners, width + 8, 2 * cap), BF)
    sent = call(send_kernel, message, table, asked, flops=2 * rows * slots * high)
    got = exchange(sent, "item")
    back, user_grad = call(
        functools.partial(triple_kernel, users=users),
        [message, shape((users, w2), F32)],
        got,
        user_rows,
        pos,
        neg,
        uid,
        scratch=[
            pltpu.VMEM((high, slots), BF),
            pltpu.VMEM((slots, triples), BF),
            pltpu.VMEM((2 * high, triples), BF),
            pltpu.VMEM((2 * w2, triples), BF),
        ],
        limit=40,
        flops=6 * slots * triples * high,
    )
    returned = exchange(back, "item")
    tiles = width // 8 * (feats // 128)
    chunk = -(-tiles // owners) * 8
    lat_grad, bias_grad, term = call(
        row_kernel,
        [shape((width, rows), F32), shape((1, rows), F32), shape((owners, chunk, 128), F32)],
        returned,
        asked,
        item_feat,
        scratch=[pltpu.VMEM((high, slots), BF)],
        flops=2 * rows * slots * high,
    )
    total = triples * groups * owners
    parts = exchange(term, "item")
    group_sum = call(
        functools.partial(sum_kernel, scale=1.0), shape((groups, chunk, 128), F32), parts
    )
    parts = exchange(group_sum, "batch")
    whole = call(
        functools.partial(sum_kernel, scale=1.0 / math.sqrt(total)),
        shape((owners, chunk, 128), F32),
        parts,
    )
    parts = exchange(whole, "item")
    projection_grad = call(join_kernel, shape((width, feats), F32), parts)
    return (lat_grad.T, bias_grad.reshape(rows), user_grad, projection_grad.T)


def solution(mesh):
    placed = (
        P(("batch", "item"), None),
        P(("batch", "item"), None),
        P(("batch", "item")),
        P(),
        P(("batch", "item"), None),
        P(("batch", "item")),
        P("batch", "item", None, None),
        P(("batch", "item")),
        P(("batch", "item")),
    )
    return jax.shard_map(
        on_device,
        mesh=mesh,
        in_specs=placed,
        out_specs=(
            P(("batch", "item"), None),
            P(("batch", "item")),
            P(("batch", "item"), None),
            P(),
        ),
        check_vma=False,
    )
```

```python
import functools
import math

import jax
import jax.numpy as jnp
from jax import lax
from jax.experimental import pallas as pl
from jax.experimental.pallas import tpu as pltpu
from jax.sharding import PartitionSpec as P

BF = jnp.bfloat16
F32 = jnp.float32
VM = pl.BlockSpec(memory_space=pltpu.VMEM)
NN = (((1,), (0,)), ((), ()))
NT = (((1,), (1,)), ((), ()))
MIB = 1024 * 1024


def mm(a, b, dims=NN):
    return lax.dot_general(a, b, dims, preferred_element_type=F32)


def split(x):
    hi = x.astype(BF)
    return hi, (x - hi.astype(F32)).astype(BF)


def matches(rows, index):
    shape16 = (16, index.shape[1])
    index = jnp.broadcast_to(index, shape16).astype(jnp.int16)
    line = lax.broadcasted_iota(jnp.int32, shape16, 0).astype(jnp.int16)
    return [line + jnp.int16(s) == index for s in range(0, rows, 16)]


def one_hot(rows, index):
    one, zero = jnp.ones((16, index.shape[1]), BF), jnp.zeros((16, index.shape[1]), BF)
    return jnp.concatenate([jnp.where(m, one, zero) for m in matches(rows, index)], axis=0)


def signed_hot(rows, plus, minus):
    same = plus == minus
    one, zero = jnp.ones((16, plus.shape[1]), BF), jnp.zeros((16, plus.shape[1]), BF)
    up = matches(rows, jnp.where(same, -1, plus))
    down = matches(rows, jnp.where(same, -1, minus))
    return jnp.concatenate(
        [jnp.where(p, one, jnp.where(m, -one, zero)) for p, m in zip(up, down)], axis=0
    )


def lane_index(ref, first, count):
    return jnp.concatenate([ref[r : r + 1, :] for r in range(first, first + count)], axis=1)


def fold(block):
    half = block.shape[0] // 2
    return jnp.concatenate([block[:half], block[half:]], axis=1)


def widen(block):
    return jnp.concatenate([block, jnp.zeros(block.shape, F32)], axis=1)


def pair(ref, o, lines, side, cap):
    cols = slice(side * cap, (side + 1) * cap)
    a, b = ref[o, lines, :].astype(F32), ref[o + 1, lines, :].astype(F32)
    return jnp.concatenate([a[:, cols], b[:, cols]], axis=1)


def table_kernel(feat_ref, lat_ref, bias_ref, proj_ref, out_ref):
    width, rows = lat_ref.shape
    out_ref[0:width, :] = lat_ref[...]
    out_ref[width : 2 * width, :] = mm(proj_ref[...], feat_ref[...], NT).astype(BF)
    first = lax.broadcasted_iota(jnp.int32, (16, rows), 0) == 0
    bias = jnp.where(first, bias_ref[...].astype(F32), 0.0)
    out_ref[2 * width :, :] = bias.astype(BF)


def send_kernel(table_ref, asked_ref, out_ref):
    owners, cap = asked_ref.shape
    rows = table_ref.shape[1]
    w2 = table_ref.shape[0] - 16
    table = table_ref[...]
    for o in range(0, owners, 4):
        hot = one_hot(rows, lane_index(asked_ref, o, 4))
        got = mm(table, hot)
        for k in range(4):
            block = got[:, k * cap : (k + 1) * cap]
            out_ref[o + k, 0 : w2 // 2, :] = fold(block[:w2]).astype(BF)
            out_ref[o + k, w2 // 2 :, :] = widen(block[w2 : w2 + 8]).astype(BF)


def hot_kernel(asked_ref, out_ref):
    for o in range(0, asked_ref.shape[0], 4):
        index = lane_index(asked_ref, o, 4)
        n = index.shape[1]
        out_ref[:, o // 4 * n : (o // 4 + 1) * n] = one_hot(out_ref.shape[0], index)


def user_kernel(user_ref, uid_ref, out_ref):
    users = user_ref.shape[0]
    table = jnp.transpose(user_ref[...].astype(F32)).astype(BF)
    step = uid_ref.shape[1]
    for r in range(0, uid_ref.shape[0], 2):
        hot = one_hot(users, lane_index(uid_ref, r, 2))
        out_ref[:, r * step : (r + 2) * step] = mm(table, hot).astype(BF)


def flatten(in_ref, flat, cap):
    owners, width = in_ref.shape[0], in_ref.shape[1] - 8
    for o in range(0, owners, 2):
        cols = slice(o * cap, (o + 2) * cap)
        flat[0:width, cols] = pair(in_ref, o, slice(0, width), 0, cap).astype(BF)
        flat[width : 2 * width, cols] = pair(in_ref, o, slice(0, width), 1, cap).astype(BF)
        bias = pair(in_ref, o, slice(width, width + 8), 0, cap)
        bias = jnp.concatenate([bias, jnp.zeros(bias.shape, F32)], axis=0)
        flat[2 * width :, cols] = bias.astype(BF)


def triple_kernel(
    got_ref, user_ref, uid_ref, pos_ref, neg_ref, send_ref, ugrad_ref, flat, diff, grad, ugd
):
    owners, cap = got_ref.shape[0], got_ref.shape[2] // 2
    width = got_ref.shape[1] - 8
    w2 = 2 * width
    high = w2 + 16
    slots = owners * cap
    triples = user_ref.shape[1]
    users = ugrad_ref.shape[0]
    flatten(got_ref, flat, cap)
    step = 2 * pos_ref.shape[1]
    table = flat[...]
    for r in range(0, pos_ref.shape[0], 2):
        cols = slice(r // 2 * step, (r // 2 + 1) * step)
        diff[:, cols] = signed_hot(slots, lane_index(pos_ref, r, 2), lane_index(neg_ref, r, 2))
        delta = mm(table, diff[:, cols])
        u = user_ref[:, cols].astype(F32)
        x = jnp.sum(u * delta[:w2], axis=0, keepdims=True) + delta[w2 : w2 + 1]
        g = -jax.nn.sigmoid(-x)
        hi, lo = split(g * u)
        first = lax.broadcasted_iota(jnp.int32, (16, step), 0) == 0
        bhi, blo = split(jnp.where(first, g, 0.0))
        grad[0:w2, cols] = hi
        grad[w2:high, cols] = bhi
        grad[high : high + w2, cols] = lo
        grad[high + w2 :, cols] = blo
        hi, lo = split(g * delta[:w2])
        ugd[0:w2, cols] = hi
        ugd[w2:, cols] = lo
    both = grad[...]
    for o in range(0, owners, 4):
        out = mm(both, diff[o * cap : (o + 4) * cap, :], NT)
        out = out[:high] + out[high:]
        for k in range(4):
            block = out[:, k * cap : (k + 1) * cap]
            send_ref[o + k, 0:width, :] = fold(block[:w2]).astype(BF)
            send_ref[o + k, width:, :] = widen(block[w2 : w2 + 8]).astype(BF)
    hot = one_hot(users, lane_index(uid_ref, 0, uid_ref.shape[0]))
    both = mm(hot, ugd[...], NT)
    ugrad_ref[...] = both[:, :w2] + both[:, w2:]


def term_kernel(back_ref, hot_ref, feat_ref, out_ref, flat):
    owners, cap = back_ref.shape[0], back_ref.shape[2] // 2
    width = back_ref.shape[1] - 8
    for o in range(0, owners, 2):
        cols = slice(o * cap, (o + 2) * cap)
        flat[:, cols] = pair(back_ref, o, slice(0, width), 1, cap).astype(BF)
    hi, lo = split(mm(flat[...], hot_ref[...], NT))
    both = mm(jnp.concatenate([hi, lo], axis=0), feat_ref[...])
    term = both[:width] + both[width:]
    across = term.shape[1] // 128
    tiles = width // 8 * across
    per = out_ref.shape[1] // 8
    for t in range(owners * per):
        o, k = divmod(t, per)
        i, j = divmod(t, across)
        tile = jnp.zeros((8, 128), F32)
        if t < tiles:
            tile = term[8 * i : 8 * i + 8, 128 * j : 128 * j + 128]
        out_ref[o, 8 * k : 8 * k + 8, :] = tile


def row_kernel(back_ref, hot_ref, lat_ref, bias_ref, flat):
    owners, cap = back_ref.shape[0], back_ref.shape[2] // 2
    width = lat_ref.shape[0]
    for o in range(0, owners, 2):
        cols = slice(o * cap, (o + 2) * cap)
        flat[0:width, cols] = pair(back_ref, o, slice(0, width), 0, cap).astype(BF)
        bias = pair(back_ref, o, slice(width, width + 8), 0, cap)
        flat[width:, cols] = jnp.concatenate([bias, jnp.zeros(bias.shape, F32)], axis=0).astype(BF)
    total = mm(flat[...], hot_ref[...], NT)
    lat_ref[...] = total[:width]
    bias_ref[...] = total[width : width + 1]


def sum_kernel(in_ref, out_ref, *, scale):
    total = in_ref[0].astype(F32)
    for k in range(1, in_ref.shape[0]):
        total = total + in_ref[k].astype(F32)
    out_ref[...] = jnp.broadcast_to((total * scale)[None], out_ref.shape).astype(out_ref.dtype)


def join_kernel(in_ref, out_ref):
    across = out_ref.shape[1] // 128
    per = in_ref.shape[1] // 8
    for o in range(out_ref.shape[0] // 8 * across // per):
        block = in_ref[o].astype(F32)
        for k in range(per):
            i, j = divmod(o * per + k, across)
            out_ref[8 * i : 8 * i + 8, 128 * j : 128 * j + 128] = block[8 * k : 8 * k + 8]


def call(kernel, out, *args, scratch=(), limit=8, flops=0, moved=0, **more):
    many = isinstance(out, (list, tuple))
    more.setdefault("in_specs", [VM] * len(args))
    more.setdefault("out_specs", [VM] * len(out) if many else VM)
    return pl.pallas_call(
        kernel,
        out_shape=out,
        scratch_shapes=list(scratch),
        compiler_params=pltpu.CompilerParams(vmem_limit_bytes=limit * MIB),
        cost_estimate=pl.CostEstimate(flops=flops, bytes_accessed=moved, transcendentals=0),
        **more,
    )(*args)


def shape(dims, dtype):
    return jax.ShapeDtypeStruct(dims, dtype)


def exchange(x, axis):
    return lax.all_to_all(x, axis, split_axis=0, concat_axis=0, tiled=True)


def on_device(
    item_feat,
    item_latent,
    item_bias,
    projection,
    user_factors,
    user_ids,
    requests,
    pos_slot,
    neg_slot,
):
    owners = lax.axis_size("item")
    groups = lax.axis_size("batch")
    rows, feats = item_feat.shape
    width = item_latent.shape[1]
    users = user_factors.shape[0]
    cap = requests.shape[-1]
    slots = owners * cap
    triples = pos_slot.shape[0]
    w2 = 2 * width
    high = w2 + 16
    lines = triples // 128

    asked = exchange(requests.reshape(owners, cap), "item")
    table = call(
        table_kernel,
        shape((high, rows), BF),
        item_feat,
        item_latent.T,
        item_bias.reshape(1, rows),
        projection.T,
        flops=2 * rows * feats * width,
        moved=2 * rows * (feats + high),
    )
    pos = pos_slot.reshape(lines, 128)
    neg = neg_slot.reshape(lines, 128)
    uid = user_ids.reshape(lines, 128)
    user_rows = call(
        user_kernel,
        shape((w2, triples), BF),
        user_factors,
        uid,
        flops=2 * users * w2 * triples,
        moved=4 * w2 * triples,
    )
    message = shape((owners, width + 8, 2 * cap), BF)
    sent = call(send_kernel, message, table, asked, flops=2 * rows * slots * high)
    got = exchange(sent, "item")
    back, user_grad = call(
        triple_kernel,
        [message, shape((users, w2), F32)],
        got,
        user_rows,
        uid,
        pos,
        neg,
        scratch=[
            pltpu.VMEM((high, slots), BF),
            pltpu.VMEM((slots, triples), BF),
            pltpu.VMEM((2 * high, triples), BF),
            pltpu.VMEM((2 * w2, triples), BF),
        ],
        limit=24,
        flops=6 * slots * triples * high,
    )
    hot = call(
        hot_kernel,
        shape((rows, slots), BF),
        asked,
        flops=4 * slots * rows,
        moved=2 * slots * rows,
    )
    back = exchange(back, "item")
    tiles = width // 8 * (feats // 128)
    chunk = -(-tiles // owners) * 8
    term = call(
        term_kernel,
        shape((owners, chunk, 128), F32),
        back,
        hot,
        item_feat,
        scratch=[pltpu.VMEM((width, slots), BF)],
        flops=2 * rows * slots * high,
    )
    parts = exchange(term, "item")
    lat_grad, bias_grad = call(
        row_kernel,
        [shape((width, rows), F32), shape((1, rows), F32)],
        back,
        hot,
        scratch=[pltpu.VMEM((width + 16, slots), BF)],
        flops=2 * rows * slots * high,
    )
    total = triples * groups * owners
    group_sum = call(
        functools.partial(sum_kernel, scale=1.0), shape((groups, chunk, 128), BF), parts
    )
    parts = exchange(group_sum, "batch")
    whole = call(
        functools.partial(sum_kernel, scale=1.0 / math.sqrt(total)),
        shape((owners, chunk, 128), BF),
        parts,
    )
    parts = exchange(whole, "item")
    projection_grad = call(join_kernel, shape((width, feats), F32), parts)
    return (lat_grad.T, bias_grad.reshape(rows), user_grad, projection_grad.T)


def solution(mesh):
    placed = (
        P(("batch", "item"), None),
        P(("batch", "item"), None),
        P(("batch", "item")),
        P(),
        P(("batch", "item"), None),
        P(("batch", "item")),
        P("batch", "item", None, None),
        P(("batch", "item")),
        P(("batch", "item")),
    )
    return jax.shard_map(
        on_device,
        mesh=mesh,
        in_specs=placed,
        out_specs=(
            P(("batch", "item"), None),
            P(("batch", "item")),
            P(("batch", "item"), None),
            P(),
        ),
        check_vma=False,
    )
```

```python
import functools
import math

import jax
import jax.numpy as jnp
from jax import lax
from jax.experimental import pallas as pl
from jax.experimental.pallas import tpu as pltpu
from jax.sharding import PartitionSpec as P

BF = jnp.bfloat16
F32 = jnp.float32
VM = pl.BlockSpec(memory_space=pltpu.VMEM)
NN = (((1,), (0,)), ((), ()))
NT = (((1,), (1,)), ((), ()))
MIB = 1024 * 1024


def mm(a, b, dims=NN):
    return lax.dot_general(a, b, dims, preferred_element_type=F32)


def split(x):
    hi = x.astype(BF)
    return hi, (x - hi.astype(F32)).astype(BF)


def matches(rows, index):
    shape16 = (16, index.shape[1])
    index = jnp.broadcast_to(index, shape16).astype(jnp.int16)
    line = lax.broadcasted_iota(jnp.int32, shape16, 0).astype(jnp.int16)
    return [line + jnp.int16(s) == index for s in range(0, rows, 16)]


def one_hot(rows, index):
    one, zero = jnp.ones((16, index.shape[1]), BF), jnp.zeros((16, index.shape[1]), BF)
    return jnp.concatenate([jnp.where(m, one, zero) for m in matches(rows, index)], axis=0)


def signed_hot(rows, plus, minus):
    same = plus == minus
    one, zero = jnp.ones((16, plus.shape[1]), BF), jnp.zeros((16, plus.shape[1]), BF)
    up = matches(rows, jnp.where(same, -1, plus))
    down = matches(rows, jnp.where(same, -1, minus))
    return jnp.concatenate(
        [jnp.where(p, one, jnp.where(m, -one, zero)) for p, m in zip(up, down)], axis=0
    )


def lane_index(ref, first, count):
    return jnp.concatenate([ref[r : r + 1, :] for r in range(first, first + count)], axis=1)


def fold(block):
    half = block.shape[0] // 2
    return jnp.concatenate([block[:half], block[half:]], axis=1)


def widen(block):
    return jnp.concatenate([block, jnp.zeros(block.shape, F32)], axis=1)


def pair(ref, o, lines, side, cap):
    cols = slice(side * cap, (side + 1) * cap)
    a, b = ref[o, lines, :].astype(F32), ref[o + 1, lines, :].astype(F32)
    return jnp.concatenate([a[:, cols], b[:, cols]], axis=1)


def table_kernel(feat_ref, lat_ref, bias_ref, proj_ref, out_ref):
    width, rows = lat_ref.shape
    out_ref[0:width, :] = lat_ref[...]
    out_ref[width : 2 * width, :] = mm(proj_ref[...], feat_ref[...], NT).astype(BF)
    first = lax.broadcasted_iota(jnp.int32, (16, rows), 0) == 0
    bias = jnp.where(first, bias_ref[...].astype(F32), 0.0)
    out_ref[2 * width :, :] = bias.astype(BF)


def send_kernel(table_ref, asked_ref, out_ref):
    owners, cap = asked_ref.shape
    rows = table_ref.shape[1]
    w2 = table_ref.shape[0] - 16
    table = table_ref[...]
    for o in range(0, owners, 4):
        hot = one_hot(rows, lane_index(asked_ref, o, 4))
        got = mm(table, hot)
        for k in range(4):
            block = got[:, k * cap : (k + 1) * cap]
            out_ref[o + k, 0 : w2 // 2, :] = fold(block[:w2]).astype(BF)
            out_ref[o + k, w2 // 2 :, :] = widen(block[w2 : w2 + 8]).astype(BF)


def fill_hot(asked_ref, hot):
    for o in range(0, asked_ref.shape[0], 4):
        index = lane_index(asked_ref, o, 4)
        n = index.shape[1]
        hot[:, o // 4 * n : (o // 4 + 1) * n] = one_hot(hot.shape[0], index)


def flatten(in_ref, flat, cap):
    owners, width = in_ref.shape[0], in_ref.shape[1] - 8
    for o in range(0, owners, 2):
        cols = slice(o * cap, (o + 2) * cap)
        flat[0:width, cols] = pair(in_ref, o, slice(0, width), 0, cap).astype(BF)
        flat[width : 2 * width, cols] = pair(in_ref, o, slice(0, width), 1, cap).astype(BF)
        bias = pair(in_ref, o, slice(width, width + 8), 0, cap)
        bias = jnp.concatenate([bias, jnp.zeros(bias.shape, F32)], axis=0)
        flat[2 * width :, cols] = bias.astype(BF)


def triple_kernel(
    got_ref, user_ref, uid_ref, pos_ref, neg_ref, send_ref, ugrad_ref, flat, diff, grad, ugd, picked
):
    owners, cap = got_ref.shape[0], got_ref.shape[2] // 2
    width = got_ref.shape[1] - 8
    w2 = 2 * width
    high = w2 + 16
    slots = owners * cap
    users = user_ref.shape[0]
    flatten(got_ref, flat, cap)
    user_table = jnp.transpose(user_ref[...].astype(F32)).astype(BF)
    step = 2 * pos_ref.shape[1]
    table = flat[...]
    for r in range(0, pos_ref.shape[0], 2):
        cols = slice(r // 2 * step, (r // 2 + 1) * step)
        diff[:, cols] = signed_hot(slots, lane_index(pos_ref, r, 2), lane_index(neg_ref, r, 2))
        delta = mm(table, diff[:, cols])
        mine = one_hot(users, lane_index(uid_ref, r, 2))
        picked[:, cols] = mine
        u = mm(user_table, mine)
        x = jnp.sum(u * delta[:w2], axis=0, keepdims=True) + delta[w2 : w2 + 1]
        g = -jax.nn.sigmoid(-x)
        hi, lo = split(g * u)
        first = lax.broadcasted_iota(jnp.int32, (16, step), 0) == 0
        bhi, blo = split(jnp.where(first, g, 0.0))
        grad[0:w2, cols] = hi
        grad[w2:high, cols] = bhi
        grad[high : high + w2, cols] = lo
        grad[high + w2 :, cols] = blo
        hi, lo = split(g * delta[:w2])
        ugd[0:w2, cols] = hi
        ugd[w2:, cols] = lo
    both = grad[...]
    for o in range(0, owners, 4):
        out = mm(both, diff[o * cap : (o + 4) * cap, :], NT)
        out = out[:high] + out[high:]
        for k in range(4):
            block = out[:, k * cap : (k + 1) * cap]
            send_ref[o + k, 0:width, :] = fold(block[:w2]).astype(BF)
            send_ref[o + k, width:, :] = widen(block[w2 : w2 + 8]).astype(BF)
    both = mm(picked[...], ugd[...], NT)
    ugrad_ref[...] = both[:, :w2] + both[:, w2:]


def block_of(ref, o, chunks):
    _, lines, span = chunks.shape
    i, j = divmod(o, ref.shape[1] // span)
    return ref[i * lines : (i + 1) * lines, j * span : (j + 1) * span]


def term_kernel(back_ref, asked_ref, feat_ref, out_ref, flat, hot):
    fill_hot(asked_ref, hot)
    owners, cap = back_ref.shape[0], back_ref.shape[2] // 2
    width = back_ref.shape[1] - 8
    for o in range(0, owners, 2):
        cols = slice(o * cap, (o + 2) * cap)
        flat[:, cols] = pair(back_ref, o, slice(0, width), 1, cap).astype(BF)
    hi, lo = split(mm(flat[...], hot[...], NT))
    both = mm(jnp.concatenate([hi, lo], axis=0), feat_ref[...])
    term = both[:width] + both[width:]
    for o in range(owners):
        out_ref[o] = block_of(term, o, out_ref)


def row_kernel(back_ref, asked_ref, lat_ref, bias_ref, flat, hot):
    fill_hot(asked_ref, hot)
    owners, cap = back_ref.shape[0], back_ref.shape[2] // 2
    width = lat_ref.shape[0]
    for o in range(0, owners, 2):
        cols = slice(o * cap, (o + 2) * cap)
        flat[0:width, cols] = pair(back_ref, o, slice(0, width), 0, cap).astype(BF)
        bias = pair(back_ref, o, slice(width, width + 8), 0, cap)
        flat[width:, cols] = jnp.concatenate([bias, jnp.zeros(bias.shape, F32)], axis=0).astype(BF)
    total = mm(flat[...], hot[...], NT)
    lat_ref[...] = total[:width]
    bias_ref[...] = total[width : width + 1]


def sum_kernel(in_ref, out_ref, *, scale):
    total = in_ref[0].astype(F32)
    for k in range(1, in_ref.shape[0]):
        total = total + in_ref[k].astype(F32)
    out_ref[...] = jnp.broadcast_to((total * scale)[None], out_ref.shape).astype(out_ref.dtype)


def join_kernel(in_ref, out_ref):
    owners, lines, span = in_ref.shape
    across = out_ref.shape[1] // span
    for o in range(0, owners, 2 * across):
        pairs = [
            jnp.concatenate([in_ref[o + j].astype(F32), in_ref[o + across + j].astype(F32)], axis=0)
            for j in range(across)
        ]
        i = o // across * lines
        for j in range(across):
            out_ref[i : i + 2 * lines, j * span : (j + 1) * span] = pairs[j]


def call(kernel, out, *args, scratch=(), limit=8, flops=0, moved=0, **more):
    many = isinstance(out, (list, tuple))
    more.setdefault("in_specs", [VM] * len(args))
    more.setdefault("out_specs", [VM] * len(out) if many else VM)
    return pl.pallas_call(
        kernel,
        out_shape=out,
        scratch_shapes=list(scratch),
        compiler_params=pltpu.CompilerParams(vmem_limit_bytes=limit * MIB),
        cost_estimate=pl.CostEstimate(flops=flops, bytes_accessed=moved, transcendentals=0),
        **more,
    )(*args)


def shape(dims, dtype):
    return jax.ShapeDtypeStruct(dims, dtype)


def exchange(x, axis):
    return lax.all_to_all(x, axis, split_axis=0, concat_axis=0, tiled=True)


def on_device(
    item_feat,
    item_latent,
    item_bias,
    projection,
    user_factors,
    user_ids,
    requests,
    pos_slot,
    neg_slot,
):
    owners = lax.axis_size("item")
    groups = lax.axis_size("batch")
    rows, feats = item_feat.shape
    width = item_latent.shape[1]
    users = user_factors.shape[0]
    cap = requests.shape[-1]
    slots = owners * cap
    triples = pos_slot.shape[0]
    w2 = 2 * width
    high = w2 + 16
    lines = triples // 128

    asked = exchange(requests.reshape(owners, cap), "item")
    pos = pos_slot.reshape(lines, 128)
    neg = neg_slot.reshape(lines, 128)
    uid = user_ids.reshape(lines, 128)
    table = call(
        table_kernel,
        shape((high, rows), BF),
        item_feat,
        item_latent.T,
        item_bias.reshape(1, rows),
        projection.T,
        flops=2 * rows * feats * width,
        moved=2 * rows * (feats + high),
    )
    message = shape((owners, width + 8, 2 * cap), BF)
    sent = call(send_kernel, message, table, asked, flops=2 * rows * slots * high)
    got = exchange(sent, "item")
    back, user_grad = call(
        triple_kernel,
        [message, shape((users, w2), F32)],
        got,
        user_factors,
        uid,
        pos,
        neg,
        scratch=[
            pltpu.VMEM((high, slots), BF),
            pltpu.VMEM((slots, triples), BF),
            pltpu.VMEM((2 * high, triples), BF),
            pltpu.VMEM((2 * w2, triples), BF),
            pltpu.VMEM((users, triples), BF),
        ],
        limit=24,
        flops=6 * slots * triples * high,
    )
    back = exchange(back, "item")
    lines = 4
    chunk = (lines, width * feats // owners // lines)
    term = call(
        term_kernel,
        shape((owners, *chunk), F32),
        back,
        asked,
        item_feat,
        scratch=[pltpu.VMEM((width, slots), BF), pltpu.VMEM((rows, slots), BF)],
        flops=2 * rows * slots * high,
    )
    parts = exchange(term, "item")
    lat_grad, bias_grad = call(
        row_kernel,
        [shape((width, rows), F32), shape((1, rows), F32)],
        back,
        asked,
        scratch=[pltpu.VMEM((width + 16, slots), BF), pltpu.VMEM((rows, slots), BF)],
        flops=2 * rows * slots * high,
    )
    total = triples * groups * owners
    group_sum = call(
        functools.partial(sum_kernel, scale=1.0), shape((groups, *chunk), BF), parts
    )
    parts = exchange(group_sum, "batch")
    whole = call(
        functools.partial(sum_kernel, scale=1.0 / math.sqrt(total)),
        shape((owners, *chunk), BF),
        parts,
    )
    parts = exchange(whole, "item")
    projection_grad = call(join_kernel, shape((width, feats), F32), parts)
    return (lat_grad.T, bias_grad.reshape(rows), user_grad, projection_grad.T)


def solution(mesh):
    placed = (
        P(("batch", "item"), None),
        P(("batch", "item"), None),
        P(("batch", "item")),
        P(),
        P(("batch", "item"), None),
        P(("batch", "item")),
        P("batch", "item", None, None),
        P(("batch", "item")),
        P(("batch", "item")),
    )
    return jax.shard_map(
        on_device,
        mesh=mesh,
        in_specs=placed,
        out_specs=(
            P(("batch", "item"), None),
            P(("batch", "item")),
            P(("batch", "item"), None),
            P(),
        ),
        check_vma=False,
    )
```

```python
import functools
import math

import jax
import jax.numpy as jnp
from jax import lax
from jax.experimental import pallas as pl
from jax.experimental.pallas import tpu as pltpu
from jax.sharding import PartitionSpec as P

BF = jnp.bfloat16
F32 = jnp.float32
VM = pl.BlockSpec(memory_space=pltpu.VMEM)
ANY = pl.BlockSpec(memory_space=pl.ANY)
NN = (((1,), (0,)), ((), ()))
NT = (((1,), (1,)), ((), ()))
MIB = 1024 * 1024


def mm(a, b, dims=NN):
    return lax.dot_general(a, b, dims, preferred_element_type=F32)


def split(x):
    hi = x.astype(BF)
    return hi, (x - hi.astype(F32)).astype(BF)


def matches(rows, index):
    shape16 = (16, index.shape[1])
    index = jnp.broadcast_to(index, shape16).astype(jnp.int16)
    line = lax.broadcasted_iota(jnp.int32, shape16, 0).astype(jnp.int16)
    return [line + jnp.int16(s) == index for s in range(0, rows, 16)]


def one_hot(rows, index):
    one, zero = jnp.ones((16, index.shape[1]), BF), jnp.zeros((16, index.shape[1]), BF)
    return jnp.concatenate([jnp.where(m, one, zero) for m in matches(rows, index)], axis=0)


def signed_hot(rows, plus, minus):
    same = plus == minus
    one, zero = jnp.ones((16, plus.shape[1]), BF), jnp.zeros((16, plus.shape[1]), BF)
    up = matches(rows, jnp.where(same, -1, plus))
    down = matches(rows, jnp.where(same, -1, minus))
    return jnp.concatenate(
        [jnp.where(p, one, jnp.where(m, -one, zero)) for p, m in zip(up, down)], axis=0
    )


def lane_index(ref, first, count):
    return jnp.concatenate([ref[r : r + 1, :] for r in range(first, first + count)], axis=1)


def fold(block):
    half = block.shape[0] // 2
    return jnp.concatenate([block[:half], block[half:]], axis=1)


def widen(block):
    return jnp.concatenate([block, jnp.zeros(block.shape, F32)], axis=1)


def pair(ref, o, lines, side, cap):
    cols = slice(side * cap, (side + 1) * cap)
    a, b = ref[o, lines, :].astype(F32), ref[o + 1, lines, :].astype(F32)
    return jnp.concatenate([a[:, cols], b[:, cols]], axis=1)


def table_kernel(feat_ref, lat_ref, bias_ref, proj_ref, out_ref):
    width, rows = lat_ref.shape
    out_ref[0:width, :] = lat_ref[...]
    out_ref[width : 2 * width, :] = mm(proj_ref[...], feat_ref[...], NT).astype(BF)
    first = lax.broadcasted_iota(jnp.int32, (16, rows), 0) == 0
    bias = jnp.where(first, bias_ref[...].astype(F32), 0.0)
    out_ref[2 * width :, :] = bias.astype(BF)


def send_kernel(table_ref, asked_ref, out_ref):
    owners, cap = asked_ref.shape
    rows = table_ref.shape[1]
    w2 = table_ref.shape[0] - 16
    table = table_ref[...]
    for o in range(0, owners, 4):
        hot = one_hot(rows, lane_index(asked_ref, o, 4))
        got = mm(table, hot)
        for k in range(4):
            block = got[:, k * cap : (k + 1) * cap]
            out_ref[o + k, 0 : w2 // 2, :] = fold(block[:w2]).astype(BF)
            out_ref[o + k, w2 // 2 :, :] = widen(block[w2 : w2 + 8]).astype(BF)


def flatten(in_ref, flat, cap):
    owners, width = in_ref.shape[0], in_ref.shape[1] - 8
    for o in range(0, owners, 2):
        cols = slice(o * cap, (o + 2) * cap)
        flat[0:width, cols] = pair(in_ref, o, slice(0, width), 0, cap).astype(BF)
        flat[width : 2 * width, cols] = pair(in_ref, o, slice(0, width), 1, cap).astype(BF)
        bias = pair(in_ref, o, slice(width, width + 8), 0, cap)
        bias = jnp.concatenate([bias, jnp.zeros(bias.shape, F32)], axis=0)
        flat[2 * width :, cols] = bias.astype(BF)


def triple_kernel(
    got_ref, user_ref, uid_ref, pos_ref, neg_ref, send_ref, ugrad_out, flat, diff, grad, ugd, picked, ugrad, sem
):
    owners, cap = got_ref.shape[0], got_ref.shape[2] // 2
    width = got_ref.shape[1] - 8
    w2 = 2 * width
    high = w2 + 16
    slots = owners * cap
    users = user_ref.shape[0]
    flatten(got_ref, flat, cap)
    user_table = jnp.transpose(user_ref[...].astype(F32)).astype(BF)
    step = 2 * pos_ref.shape[1]
    table = flat[...]
    for r in range(0, pos_ref.shape[0], 2):
        cols = slice(r // 2 * step, (r // 2 + 1) * step)
        diff[:, cols] = signed_hot(slots, lane_index(pos_ref, r, 2), lane_index(neg_ref, r, 2))
        delta = mm(table, diff[:, cols])
        mine = one_hot(users, lane_index(uid_ref, r, 2))
        picked[:, cols] = mine
        u = mm(user_table, mine)
        x = jnp.sum(u * delta[:w2], axis=0, keepdims=True) + delta[w2 : w2 + 1]
        g = -jax.nn.sigmoid(-x)
        hi, lo = split(g * u)
        first = lax.broadcasted_iota(jnp.int32, (16, step), 0) == 0
        bhi, blo = split(jnp.where(first, g, 0.0))
        grad[0:w2, cols] = hi
        grad[w2:high, cols] = bhi
        grad[high : high + w2, cols] = lo
        grad[high + w2 :, cols] = blo
        hi, lo = split(g * delta[:w2])
        ugd[0:w2, cols] = hi
        ugd[w2:, cols] = lo
    both = mm(picked[...], ugd[...], NT)
    ugrad[...] = both[:, :w2] + both[:, w2:]
    copy = pltpu.make_async_copy(ugrad, ugrad_out, sem)
    copy.start()
    both = grad[...]
    for o in range(0, owners, 4):
        out = mm(both, diff[o * cap : (o + 4) * cap, :], NT)
        out = out[:high] + out[high:]
        for k in range(4):
            block = out[:, k * cap : (k + 1) * cap]
            send_ref[o + k, 0:width, :] = fold(block[:w2]).astype(BF)
            send_ref[o + k, width:, :] = widen(block[w2 : w2 + 8]).astype(BF)
    copy.wait()


def block_of(ref, o, chunks):
    _, lines, span = chunks.shape
    i, j = divmod(o, ref.shape[1] // span)
    return ref[i * lines : (i + 1) * lines, j * span : (j + 1) * span]


def term_kernel(
    back_ref, asked_ref, feat_ref, lat_out, bias_out, out_ref, lat_ref, bias_ref, sems
):
    owners, cap = asked_ref.shape
    width = back_ref.shape[1] - 8
    rows = feat_ref.shape[0]
    total = jnp.zeros((2 * width + 16, rows), F32)
    for o in range(0, owners, 8):
        parts = []
        for k in range(o, o + 8, 2):
            bias = pair(back_ref, k, slice(width, width + 8), 0, cap)
            both = [pair(back_ref, k, slice(0, width), side, cap) for side in range(2)]
            parts.append(jnp.concatenate([*both, bias, jnp.zeros(bias.shape, F32)], axis=0))
        part = jnp.concatenate(parts, axis=1).astype(BF)
        total = total + mm(part, one_hot(rows, lane_index(asked_ref, o, 8)), NT)
    lat_ref[...] = total[:width]
    bias_ref[...] = total[2 * width : 2 * width + 1]
    copies = [
        pltpu.make_async_copy(lat_ref, lat_out, sems.at[0]),
        pltpu.make_async_copy(bias_ref, bias_out, sems.at[1]),
    ]
    for copy in copies:
        copy.start()
    total = total[width : 2 * width]
    hi, lo = split(total)
    both = mm(jnp.concatenate([hi, lo], axis=0), feat_ref[...])
    term = both[:width] + both[width:]
    for o in range(owners):
        out_ref[o] = block_of(term, o, out_ref)
    for copy in copies:
        copy.wait()


def sum_kernel(in_ref, out_ref, *, scale):
    total = in_ref[0].astype(F32)
    for k in range(1, in_ref.shape[0]):
        total = total + in_ref[k].astype(F32)
    out_ref[...] = jnp.broadcast_to((total * scale)[None], out_ref.shape).astype(out_ref.dtype)


def join_kernel(in_ref, out_ref):
    owners, lines, span = in_ref.shape
    across = out_ref.shape[1] // span
    for o in range(0, owners, 2 * across):
        pairs = [
            jnp.concatenate([in_ref[o + j].astype(F32), in_ref[o + across + j].astype(F32)], axis=0)
            for j in range(across)
        ]
        i = o // across * lines
        for j in range(across):
            out_ref[i : i + 2 * lines, j * span : (j + 1) * span] = pairs[j]


def call(kernel, out, *args, scratch=(), limit=8, flops=0, moved=0, **more):
    many = isinstance(out, (list, tuple))
    more.setdefault("in_specs", [VM] * len(args))
    more.setdefault("out_specs", [VM] * len(out) if many else VM)
    return pl.pallas_call(
        kernel,
        out_shape=out,
        scratch_shapes=list(scratch),
        compiler_params=pltpu.CompilerParams(vmem_limit_bytes=limit * MIB),
        cost_estimate=pl.CostEstimate(flops=flops, bytes_accessed=moved, transcendentals=0),
        **more,
    )(*args)


def shape(dims, dtype):
    return jax.ShapeDtypeStruct(dims, dtype)


def exchange(x, axis):
    return lax.all_to_all(x, axis, split_axis=0, concat_axis=0, tiled=True)


def on_device(
    item_feat,
    item_latent,
    item_bias,
    projection,
    user_factors,
    user_ids,
    requests,
    pos_slot,
    neg_slot,
):
    owners = lax.axis_size("item")
    groups = lax.axis_size("batch")
    rows, feats = item_feat.shape
    width = item_latent.shape[1]
    users = user_factors.shape[0]
    cap = requests.shape[-1]
    slots = owners * cap
    triples = pos_slot.shape[0]
    w2 = 2 * width
    high = w2 + 16
    lines = triples // 128

    asked = exchange(requests.reshape(owners, cap), "item")
    pos = pos_slot.reshape(lines, 128)
    neg = neg_slot.reshape(lines, 128)
    uid = user_ids.reshape(lines, 128)
    table = call(
        table_kernel,
        shape((high, rows), BF),
        item_feat,
        item_latent.T,
        item_bias.reshape(1, rows),
        projection.T,
        flops=2 * rows * feats * width,
        moved=2 * rows * (feats + high),
    )
    message = shape((owners, width + 8, 2 * cap), BF)
    sent = call(send_kernel, message, table, asked, flops=2 * rows * slots * high)
    got = exchange(sent, "item")
    back, user_grad = call(
        triple_kernel,
        [message, shape((users, w2), F32)],
        got,
        user_factors,
        uid,
        pos,
        neg,
        scratch=[
            pltpu.VMEM((high, slots), BF),
            pltpu.VMEM((slots, triples), BF),
            pltpu.VMEM((2 * high, triples), BF),
            pltpu.VMEM((2 * w2, triples), BF),
            pltpu.VMEM((users, triples), BF),
            pltpu.VMEM((users, w2), F32),
            pltpu.SemaphoreType.DMA,
        ],
        out_specs=[VM, ANY],
        limit=24,
        flops=6 * slots * triples * high,
    )
    back = exchange(back, "item")
    lines = 4
    chunk = (lines, width * feats // owners // lines)
    lat_grad, bias_grad, term = call(
        term_kernel,
        [shape((width, rows), F32), shape((1, rows), F32), shape((owners, *chunk), F32)],
        back,
        asked,
        item_feat,
        out_specs=[ANY, ANY, VM],
        scratch=[
            pltpu.VMEM((width, rows), F32),
            pltpu.VMEM((1, rows), F32),
            pltpu.SemaphoreType.DMA((2,)),
        ],
        flops=2 * rows * slots * high,
    )
    parts = exchange(term, "item")
    total = triples * groups * owners
    group_sum = call(
        functools.partial(sum_kernel, scale=1.0), shape((groups, *chunk), BF), parts
    )
    parts = exchange(group_sum, "batch")
    whole = call(
        functools.partial(sum_kernel, scale=1.0 / math.sqrt(total)),
        shape((owners, *chunk), BF),
        parts,
    )
    parts = exchange(whole, "item")
    projection_grad = call(join_kernel, shape((width, feats), F32), parts)
    return (lat_grad.T, bias_grad.reshape(rows), user_grad, projection_grad.T)


def solution(mesh):
    placed = (
        P(("batch", "item"), None),
        P(("batch", "item"), None),
        P(("batch", "item")),
        P(),
        P(("batch", "item"), None),
        P(("batch", "item")),
        P("batch", "item", None, None),
        P(("batch", "item")),
        P(("batch", "item")),
    )
    return jax.shard_map(
        on_device,
        mesh=mesh,
        in_specs=placed,
        out_specs=(
            P(("batch", "item"), None),
            P(("batch", "item")),
            P(("batch", "item"), None),
            P(),
        ),
        check_vma=False,
    )
```

```python
import functools
import math

import jax
import jax.numpy as jnp
from jax import lax
from jax.experimental import pallas as pl
from jax.experimental.pallas import tpu as pltpu
from jax.sharding import PartitionSpec as P

BF = jnp.bfloat16
F32 = jnp.float32
VM = pl.BlockSpec(memory_space=pltpu.VMEM)
ANY = pl.BlockSpec(memory_space=pl.ANY)
NN = (((1,), (0,)), ((), ()))
NT = (((1,), (1,)), ((), ()))
MIB = 1024 * 1024


def mm(a, b, dims=NN):
    return lax.dot_general(a, b, dims, preferred_element_type=F32)


def split(x):
    hi = x.astype(BF)
    return hi, (x - hi.astype(F32)).astype(BF)


def matches(rows, index):
    shape16 = (16, index.shape[1])
    index = jnp.broadcast_to(index, shape16).astype(jnp.int16)
    line = lax.broadcasted_iota(jnp.int32, shape16, 0).astype(jnp.int16)
    return [line + jnp.int16(s) == index for s in range(0, rows, 16)]


def one_hot(rows, index):
    one, zero = jnp.ones((16, index.shape[1]), BF), jnp.zeros((16, index.shape[1]), BF)
    return jnp.concatenate([jnp.where(m, one, zero) for m in matches(rows, index)], axis=0)


def signed_hot(rows, plus, minus):
    same = plus == minus
    one, zero = jnp.ones((16, plus.shape[1]), BF), jnp.zeros((16, plus.shape[1]), BF)
    up = matches(rows, jnp.where(same, -1, plus))
    down = matches(rows, jnp.where(same, -1, minus))
    return jnp.concatenate(
        [jnp.where(p, one, jnp.where(m, -one, zero)) for p, m in zip(up, down)], axis=0
    )


def lane_index(ref, first, count):
    return jnp.concatenate([ref[r : r + 1, :] for r in range(first, first + count)], axis=1)


def fold(block):
    half = block.shape[0] // 2
    return jnp.concatenate([block[:half], block[half:]], axis=1)


def widen(block):
    return jnp.concatenate([block, jnp.zeros(block.shape, F32)], axis=1)


def pair(ref, o, lines, side, cap):
    cols = slice(side * cap, (side + 1) * cap)
    a, b = ref[o, lines, :].astype(F32), ref[o + 1, lines, :].astype(F32)
    return jnp.concatenate([a[:, cols], b[:, cols]], axis=1)


def table_kernel(feat_ref, lat_ref, bias_ref, proj_ref, out_ref):
    width, rows = lat_ref.shape
    out_ref[0:width, :] = lat_ref[...]
    out_ref[width : 2 * width, :] = mm(proj_ref[...], feat_ref[...], NT).astype(BF)
    first = lax.broadcasted_iota(jnp.int32, (16, rows), 0) == 0
    bias = jnp.where(first, bias_ref[...].astype(F32), 0.0)
    out_ref[2 * width :, :] = bias.astype(BF)


def send_kernel(table_ref, asked_ref, out_ref):
    owners, cap = asked_ref.shape
    rows = table_ref.shape[1]
    w2 = table_ref.shape[0] - 16
    table = table_ref[...]
    for o in range(0, owners, 4):
        hot = one_hot(rows, lane_index(asked_ref, o, 4))
        got = mm(table, hot)
        for k in range(4):
            block = got[:, k * cap : (k + 1) * cap]
            out_ref[o + k, 0 : w2 // 2, :] = fold(block[:w2]).astype(BF)
            out_ref[o + k, w2 // 2 :, :] = widen(block[w2 : w2 + 8]).astype(BF)


def flatten(in_ref, flat, cap):
    owners, width = in_ref.shape[0], in_ref.shape[1] - 8
    for o in range(0, owners, 2):
        cols = slice(o * cap, (o + 2) * cap)
        flat[0:width, cols] = pair(in_ref, o, slice(0, width), 0, cap).astype(BF)
        flat[width : 2 * width, cols] = pair(in_ref, o, slice(0, width), 1, cap).astype(BF)
        bias = pair(in_ref, o, slice(width, width + 8), 0, cap)
        bias = jnp.concatenate([bias, jnp.zeros(bias.shape, F32)], axis=0)
        flat[2 * width :, cols] = bias.astype(BF)


def triple_kernel(
    got_ref, user_ref, uid_ref, pos_ref, neg_ref, send_ref, ugrad_out, flat, diff, grad, ugd, picked, ugrad, sem
):
    owners, cap = got_ref.shape[0], got_ref.shape[2] // 2
    width = got_ref.shape[1] - 8
    w2 = 2 * width
    high = w2 + 16
    slots = owners * cap
    users = user_ref.shape[0]
    flatten(got_ref, flat, cap)
    user_table = jnp.transpose(user_ref[...].astype(F32)).astype(BF)
    step = 2 * pos_ref.shape[1]
    table = flat[...]
    for r in range(0, pos_ref.shape[0], 2):
        cols = slice(r // 2 * step, (r // 2 + 1) * step)
        diff[:, cols] = signed_hot(slots, lane_index(pos_ref, r, 2), lane_index(neg_ref, r, 2))
        delta = mm(table, diff[:, cols])
        mine = one_hot(users, lane_index(uid_ref, r, 2))
        picked[:, cols] = mine
        u = mm(user_table, mine)
        x = jnp.sum(u * delta[:w2], axis=0, keepdims=True) + delta[w2 : w2 + 1]
        g = -jax.nn.sigmoid(-x)
        hi, lo = split(g * u)
        first = lax.broadcasted_iota(jnp.int32, (16, step), 0) == 0
        bhi, blo = split(jnp.where(first, g, 0.0))
        grad[0:w2, cols] = hi
        grad[w2:high, cols] = bhi
        grad[high : high + w2, cols] = lo
        grad[high + w2 :, cols] = blo
        hi, lo = split(g * delta[:w2])
        ugd[0:w2, cols] = hi
        ugd[w2:, cols] = lo
    both = mm(picked[...], ugd[...], NT)
    ugrad[...] = both[:, :w2] + both[:, w2:]
    copy = pltpu.make_async_copy(ugrad, ugrad_out, sem)
    copy.start()
    both = grad[...]
    for o in range(0, owners, 4):
        out = mm(both, diff[o * cap : (o + 4) * cap, :], NT)
        out = out[:high] + out[high:]
        for k in range(4):
            block = out[:, k * cap : (k + 1) * cap]
            send_ref[o + k, 0:width, :] = fold(block[:w2]).astype(BF)
            send_ref[o + k, width:, :] = widen(block[w2 : w2 + 8]).astype(BF)
    copy.wait()


def block_of(ref, o, chunks):
    _, lines, span = chunks.shape
    i, j = divmod(o, ref.shape[1] // span)
    return ref[i * lines : (i + 1) * lines, j * span : (j + 1) * span]


def term_kernel(back_ref, asked_ref, feat_ref, lat_ref, bias_ref, out_ref):
    owners, cap = asked_ref.shape
    width = back_ref.shape[1] - 8
    rows = feat_ref.shape[0]
    total = jnp.zeros((2 * width + 16, rows), F32)
    for o in range(0, owners, 8):
        parts = []
        for k in range(o, o + 8, 2):
            bias = pair(back_ref, k, slice(width, width + 8), 0, cap)
            both = [pair(back_ref, k, slice(0, width), side, cap) for side in range(2)]
            parts.append(jnp.concatenate([*both, bias, jnp.zeros(bias.shape, F32)], axis=0))
        part = jnp.concatenate(parts, axis=1).astype(BF)
        total = total + mm(part, one_hot(rows, lane_index(asked_ref, o, 8)), NT)
    lat_ref[...] = total[:width]
    bias_ref[...] = total[2 * width : 2 * width + 1]
    total = total[width : 2 * width]
    hi, lo = split(total)
    both = mm(jnp.concatenate([hi, lo], axis=0), feat_ref[...])
    term = both[:width] + both[width:]
    for o in range(owners):
        out_ref[o] = block_of(term, o, out_ref)


def sum_kernel(in_ref, out_ref, *, scale):
    total = in_ref[0].astype(F32)
    for k in range(1, in_ref.shape[0]):
        total = total + in_ref[k].astype(F32)
    out_ref[...] = jnp.broadcast_to((total * scale)[None], out_ref.shape).astype(out_ref.dtype)


def join_kernel(in_ref, lat_ref, bias_ref, out_hbm, lat_hbm, bias_hbm, out_ref, sems):
    moves = [(lat_ref, lat_hbm), (bias_ref, bias_hbm), (out_ref, out_hbm)]
    copies = [pltpu.make_async_copy(a, b, sems.at[i]) for i, (a, b) in enumerate(moves)]
    for copy in copies[:2]:
        copy.start()
    owners, lines, span = in_ref.shape
    across = out_ref.shape[1] // span
    for o in range(0, owners, 2 * across):
        i = o // across * lines
        for j in range(across):
            pair = [in_ref[o + j].astype(F32), in_ref[o + across + j].astype(F32)]
            columns = slice(j * span, (j + 1) * span)
            out_ref[i : i + 2 * lines, columns] = jnp.concatenate(pair, axis=0)
    copies[2].start()
    for copy in copies:
        copy.wait()


def call(kernel, out, *args, scratch=(), limit=8, flops=0, moved=0, **more):
    many = isinstance(out, (list, tuple))
    more.setdefault("in_specs", [VM] * len(args))
    more.setdefault("out_specs", [VM] * len(out) if many else VM)
    return pl.pallas_call(
        kernel,
        out_shape=out,
        scratch_shapes=list(scratch),
        compiler_params=pltpu.CompilerParams(vmem_limit_bytes=limit * MIB),
        cost_estimate=pl.CostEstimate(flops=flops, bytes_accessed=moved, transcendentals=0),
        **more,
    )(*args)


def shape(dims, dtype):
    return jax.ShapeDtypeStruct(dims, dtype)


def exchange(x, axis):
    return lax.all_to_all(x, axis, split_axis=0, concat_axis=0, tiled=True)


def on_device(
    item_feat,
    item_latent,
    item_bias,
    projection,
    user_factors,
    user_ids,
    requests,
    pos_slot,
    neg_slot,
):
    owners = lax.axis_size("item")
    groups = lax.axis_size("batch")
    rows, feats = item_feat.shape
    width = item_latent.shape[1]
    users = user_factors.shape[0]
    cap = requests.shape[-1]
    slots = owners * cap
    triples = pos_slot.shape[0]
    w2 = 2 * width
    high = w2 + 16
    lines = triples // 128

    asked = exchange(requests.reshape(owners, cap), "item")
    pos = pos_slot.reshape(lines, 128)
    neg = neg_slot.reshape(lines, 128)
    uid = user_ids.reshape(lines, 128)
    table = call(
        table_kernel,
        shape((high, rows), BF),
        item_feat,
        item_latent.T,
        item_bias.reshape(1, rows),
        projection.T,
        flops=2 * rows * feats * width,
        moved=2 * rows * (feats + high),
    )
    message = shape((owners, width + 8, 2 * cap), BF)
    sent = call(send_kernel, message, table, asked, flops=2 * rows * slots * high)
    got = exchange(sent, "item")
    back, user_grad = call(
        triple_kernel,
        [message, shape((users, w2), F32)],
        got,
        user_factors,
        uid,
        pos,
        neg,
        scratch=[
            pltpu.VMEM((high, slots), BF),
            pltpu.VMEM((slots, triples), BF),
            pltpu.VMEM((2 * high, triples), BF),
            pltpu.VMEM((2 * w2, triples), BF),
            pltpu.VMEM((users, triples), BF),
            pltpu.VMEM((users, w2), F32),
            pltpu.SemaphoreType.DMA,
        ],
        out_specs=[VM, ANY],
        limit=24,
        flops=6 * slots * triples * high,
    )
    back = exchange(back, "item")
    lines = 4
    chunk = (lines, width * feats // owners // lines)
    lat_grad, bias_grad, term = call(
        term_kernel,
        [shape((width, rows), F32), shape((1, rows), F32), shape((owners, *chunk), F32)],
        back,
        asked,
        item_feat,
        flops=2 * rows * slots * high,
    )
    parts = exchange(term, "item")
    total = triples * groups * owners
    group_sum = call(
        functools.partial(sum_kernel, scale=1.0), shape((groups, *chunk), BF), parts
    )
    parts = exchange(group_sum, "batch")
    whole = call(
        functools.partial(sum_kernel, scale=1.0 / math.sqrt(total)),
        shape((owners, *chunk), BF),
        parts,
    )
    parts = exchange(whole, "item")
    projection_grad, lat_grad, bias_grad = call(
        join_kernel,
        [shape((width, feats), F32), shape((width, rows), F32), shape((1, rows), F32)],
        parts,
        lat_grad,
        bias_grad,
        out_specs=[ANY] * 3,
        scratch=[pltpu.VMEM((width, feats), F32), pltpu.SemaphoreType.DMA((3,))],
    )
    return (lat_grad.T, bias_grad.reshape(rows), user_grad, projection_grad.T)


def solution(mesh):
    placed = (
        P(("batch", "item"), None),
        P(("batch", "item"), None),
        P(("batch", "item")),
        P(),
        P(("batch", "item"), None),
        P(("batch", "item")),
        P("batch", "item", None, None),
        P(("batch", "item")),
        P(("batch", "item")),
    )
    return jax.shard_map(
        on_device,
        mesh=mesh,
        in_specs=placed,
        out_specs=(
            P(("batch", "item"), None),
            P(("batch", "item")),
            P(("batch", "item"), None),
            P(),
        ),
        check_vma=False,
    )
```

```python
import functools
import math

import jax
import jax.numpy as jnp
from jax import lax
from jax.experimental import pallas as pl
from jax.experimental.pallas import tpu as pltpu
from jax.sharding import PartitionSpec as P

BF = jnp.bfloat16
F32 = jnp.float32
VM = pl.BlockSpec(memory_space=pltpu.VMEM)
ANY = pl.BlockSpec(memory_space=pl.ANY)
NN = (((1,), (0,)), ((), ()))
NT = (((1,), (1,)), ((), ()))
MIB = 1024 * 1024


def mm(a, b, dims=NN):
    return lax.dot_general(a, b, dims, preferred_element_type=F32)


def split(x):
    hi = x.astype(BF)
    return hi, (x - hi.astype(F32)).astype(BF)


def matches(rows, index):
    shape16 = (16, index.shape[1])
    index = jnp.broadcast_to(index, shape16).astype(jnp.int16)
    line = lax.broadcasted_iota(jnp.int32, shape16, 0).astype(jnp.int16)
    return [line + jnp.int16(s) == index for s in range(0, rows, 16)]


def one_hot(rows, index):
    one, zero = jnp.ones((16, index.shape[1]), BF), jnp.zeros((16, index.shape[1]), BF)
    return jnp.concatenate([jnp.where(m, one, zero) for m in matches(rows, index)], axis=0)


def signed_hot(rows, plus, minus):
    same = plus == minus
    one, zero = jnp.ones((16, plus.shape[1]), BF), jnp.zeros((16, plus.shape[1]), BF)
    up = matches(rows, jnp.where(same, -1, plus))
    down = matches(rows, jnp.where(same, -1, minus))
    return jnp.concatenate(
        [jnp.where(p, one, jnp.where(m, -one, zero)) for p, m in zip(up, down)], axis=0
    )


def lane_index(ref, first, count):
    return jnp.concatenate([ref[r : r + 1, :] for r in range(first, first + count)], axis=1)


def fold(block):
    half = block.shape[0] // 2
    return jnp.concatenate([block[:half], block[half:]], axis=1)


def widen(block):
    return jnp.concatenate([block, jnp.zeros(block.shape, F32)], axis=1)


def pair(ref, o, lines, side, cap):
    cols = slice(side * cap, (side + 1) * cap)
    a, b = take(ref, o)[lines], take(ref, o + 1)[lines]
    return jnp.concatenate([a[:, cols], b[:, cols]], axis=1)


def put(ref, o, block, w2):
    _, parts, lines, span = ref.shape
    ref[o, : parts - 1] = fold(block[:w2]).astype(BF).reshape(parts - 1, lines, span)
    ref[o, parts - 1] = widen(block[w2 : w2 + lines]).astype(BF)


def width_of(ref):
    return (ref.shape[1] - 1) * ref.shape[2]


def take(ref, o):
    _, parts, lines, span = ref.shape
    full = ref[o, : parts - 1].reshape((parts - 1) * lines, span).astype(F32)
    bias = ref[o, parts - 1].astype(F32)
    return jnp.concatenate([full, bias, jnp.zeros(bias.shape, F32)], axis=0)


def table_kernel(feat_ref, lat_ref, bias_ref, proj_ref, out_ref):
    width, rows = lat_ref.shape
    out_ref[0:width, :] = lat_ref[...]
    out_ref[width : 2 * width, :] = mm(proj_ref[...], feat_ref[...], NT).astype(BF)
    first = lax.broadcasted_iota(jnp.int32, (16, rows), 0) == 0
    bias = jnp.where(first, bias_ref[...].astype(F32), 0.0)
    out_ref[2 * width :, :] = bias.astype(BF)


def send_kernel(table_ref, asked_ref, out_ref):
    owners, cap = asked_ref.shape
    rows = table_ref.shape[1]
    w2 = table_ref.shape[0] - 16
    table = table_ref[...]
    for o in range(0, owners, 4):
        hot = one_hot(rows, lane_index(asked_ref, o, 4))
        got = mm(table, hot)
        for k in range(4):
            block = got[:, k * cap : (k + 1) * cap]
            put(out_ref, o + k, block, w2)


def flatten(in_ref, flat, cap):
    owners, width = in_ref.shape[0], width_of(in_ref)
    for o in range(0, owners, 2):
        cols = slice(o * cap, (o + 2) * cap)
        flat[0:width, cols] = pair(in_ref, o, slice(0, width), 0, cap).astype(BF)
        flat[width : 2 * width, cols] = pair(in_ref, o, slice(0, width), 1, cap).astype(BF)
        bias = pair(in_ref, o, slice(width, width + 8), 0, cap)
        bias = jnp.concatenate([bias, jnp.zeros(bias.shape, F32)], axis=0)
        flat[2 * width :, cols] = bias.astype(BF)


def triple_kernel(
    got_ref, user_ref, uid_ref, pos_ref, neg_ref, send_ref, ugrad_out, flat, diff, grad, ugd, picked, ugrad, sem
):
    owners, cap = got_ref.shape[0], got_ref.shape[3] // 2
    width = width_of(got_ref)
    w2 = 2 * width
    high = w2 + 16
    slots = owners * cap
    users = user_ref.shape[0]
    flatten(got_ref, flat, cap)
    user_table = jnp.transpose(user_ref[...].astype(F32)).astype(BF)
    step = 2 * pos_ref.shape[1]
    table = flat[...]
    for r in range(0, pos_ref.shape[0], 2):
        cols = slice(r // 2 * step, (r // 2 + 1) * step)
        diff[:, cols] = signed_hot(slots, lane_index(pos_ref, r, 2), lane_index(neg_ref, r, 2))
        delta = mm(table, diff[:, cols])
        mine = one_hot(users, lane_index(uid_ref, r, 2))
        picked[:, cols] = mine
        u = mm(user_table, mine)
        x = jnp.sum(u * delta[:w2], axis=0, keepdims=True) + delta[w2 : w2 + 1]
        g = -jax.nn.sigmoid(-x)
        hi, lo = split(g * u)
        first = lax.broadcasted_iota(jnp.int32, (16, step), 0) == 0
        bhi, blo = split(jnp.where(first, g, 0.0))
        grad[0:w2, cols] = hi
        grad[w2:high, cols] = bhi
        grad[high : high + w2, cols] = lo
        grad[high + w2 :, cols] = blo
        hi, lo = split(g * delta[:w2])
        ugd[0:w2, cols] = hi
        ugd[w2:, cols] = lo
    both = mm(picked[...], ugd[...], NT)
    ugrad[...] = both[:, :w2] + both[:, w2:]
    copy = pltpu.make_async_copy(ugrad, ugrad_out, sem)
    copy.start()
    both = grad[...]
    for o in range(0, owners, 4):
        out = mm(both, diff[o * cap : (o + 4) * cap, :], NT)
        out = out[:high] + out[high:]
        for k in range(4):
            block = out[:, k * cap : (k + 1) * cap]
            put(send_ref, o + k, block, w2)
    copy.wait()


def block_of(ref, o, chunks):
    _, lines, span = chunks.shape
    i, j = divmod(o, ref.shape[1] // span)
    return ref[i * lines : (i + 1) * lines, j * span : (j + 1) * span]


def term_kernel(back_ref, asked_ref, feat_ref, lat_ref, bias_ref, out_ref):
    owners, cap = asked_ref.shape
    width = width_of(back_ref)
    rows = feat_ref.shape[0]
    total = jnp.zeros((2 * width + 16, rows), F32)
    for o in range(0, owners, 8):
        parts = []
        for k in range(o, o + 8, 2):
            bias = pair(back_ref, k, slice(width, width + 8), 0, cap)
            both = [pair(back_ref, k, slice(0, width), side, cap) for side in range(2)]
            parts.append(jnp.concatenate([*both, bias, jnp.zeros(bias.shape, F32)], axis=0))
        part = jnp.concatenate(parts, axis=1).astype(BF)
        total = total + mm(part, one_hot(rows, lane_index(asked_ref, o, 8)), NT)
    lat_ref[...] = total[:width]
    bias_ref[...] = total[2 * width : 2 * width + 1]
    total = total[width : 2 * width]
    hi, lo = split(total)
    both = mm(jnp.concatenate([hi, lo], axis=0), feat_ref[...])
    term = both[:width] + both[width:]
    for o in range(owners):
        out_ref[o] = block_of(term, o, out_ref)


def sum_kernel(in_ref, out_ref, *, scale):
    total = in_ref[0].astype(F32)
    for k in range(1, in_ref.shape[0]):
        total = total + in_ref[k].astype(F32)
    out_ref[...] = jnp.broadcast_to((total * scale)[None], out_ref.shape).astype(out_ref.dtype)


def join_kernel(in_ref, lat_ref, bias_ref, out_hbm, lat_hbm, bias_hbm, out_ref, sems):
    moves = [(lat_ref, lat_hbm), (bias_ref, bias_hbm), (out_ref, out_hbm)]
    copies = [pltpu.make_async_copy(a, b, sems.at[i]) for i, (a, b) in enumerate(moves)]
    for copy in copies[:2]:
        copy.start()
    owners, lines, span = in_ref.shape
    across = out_ref.shape[1] // span
    for o in range(0, owners, 2 * across):
        i = o // across * lines
        for j in range(across):
            pair = [in_ref[o + j].astype(F32), in_ref[o + across + j].astype(F32)]
            columns = slice(j * span, (j + 1) * span)
            out_ref[i : i + 2 * lines, columns] = jnp.concatenate(pair, axis=0)
    copies[2].start()
    for copy in copies:
        copy.wait()


def call(kernel, out, *args, scratch=(), limit=8, flops=0, moved=0, **more):
    many = isinstance(out, (list, tuple))
    more.setdefault("in_specs", [VM] * len(args))
    more.setdefault("out_specs", [VM] * len(out) if many else VM)
    return pl.pallas_call(
        kernel,
        out_shape=out,
        scratch_shapes=list(scratch),
        compiler_params=pltpu.CompilerParams(vmem_limit_bytes=limit * MIB),
        cost_estimate=pl.CostEstimate(flops=flops, bytes_accessed=moved, transcendentals=0),
        **more,
    )(*args)


def shape(dims, dtype):
    return jax.ShapeDtypeStruct(dims, dtype)


def exchange(x, axis):
    return lax.all_to_all(x, axis, split_axis=0, concat_axis=0, tiled=True)


def on_device(
    item_feat,
    item_latent,
    item_bias,
    projection,
    user_factors,
    user_ids,
    requests,
    pos_slot,
    neg_slot,
):
    owners = lax.axis_size("item")
    groups = lax.axis_size("batch")
    rows, feats = item_feat.shape
    width = item_latent.shape[1]
    users = user_factors.shape[0]
    cap = requests.shape[-1]
    slots = owners * cap
    triples = pos_slot.shape[0]
    w2 = 2 * width
    high = w2 + 16
    rows128 = triples // 128

    asked = exchange(requests.reshape(owners, cap), "item")
    pos = pos_slot.reshape(rows128, 128)
    neg = neg_slot.reshape(rows128, 128)
    uid = user_ids.reshape(rows128, 128)
    table = call(
        table_kernel,
        shape((high, rows), BF),
        item_feat,
        item_latent.T,
        item_bias.reshape(1, rows),
        projection.T,
        flops=2 * rows * feats * width,
        moved=2 * rows * (feats + high),
    )
    lines = 4
    message = shape((owners, width // lines + 1, lines, 2 * cap), BF)
    sent = call(send_kernel, message, table, asked, flops=2 * rows * slots * high)
    got = exchange(sent, "item")
    back, user_grad = call(
        triple_kernel,
        [message, shape((users, w2), F32)],
        got,
        user_factors,
        uid,
        pos,
        neg,
        scratch=[
            pltpu.VMEM((high, slots), BF),
            pltpu.VMEM((slots, triples), BF),
            pltpu.VMEM((2 * high, triples), BF),
            pltpu.VMEM((2 * w2, triples), BF),
            pltpu.VMEM((users, triples), BF),
            pltpu.VMEM((users, w2), F32),
            pltpu.SemaphoreType.DMA,
        ],
        out_specs=[VM, ANY],
        limit=24,
        flops=6 * slots * triples * high,
    )
    back = exchange(back, "item")
    chunk = (lines, width * feats // owners // lines)
    lat_grad, bias_grad, term = call(
        term_kernel,
        [shape((width, rows), F32), shape((1, rows), F32), shape((owners, *chunk), F32)],
        back,
        asked,
        item_feat,
        flops=2 * rows * slots * high,
    )
    parts = exchange(term, "item")
    total = triples * groups * owners
    group_sum = call(
        functools.partial(sum_kernel, scale=1.0), shape((groups, *chunk), BF), parts
    )
    parts = exchange(group_sum, "batch")
    whole = call(
        functools.partial(sum_kernel, scale=1.0 / math.sqrt(total)),
        shape((owners, *chunk), BF),
        parts,
    )
    parts = exchange(whole, "item")
    projection_grad, lat_grad, bias_grad = call(
        join_kernel,
        [shape((width, feats), F32), shape((width, rows), F32), shape((1, rows), F32)],
        parts,
        lat_grad,
        bias_grad,
        out_specs=[ANY] * 3,
        scratch=[pltpu.VMEM((width, feats), F32), pltpu.SemaphoreType.DMA((3,))],
    )
    return (lat_grad.T, bias_grad.reshape(rows), user_grad, projection_grad.T)


def solution(mesh):
    placed = (
        P(("batch", "item"), None),
        P(("batch", "item"), None),
        P(("batch", "item")),
        P(),
        P(("batch", "item"), None),
        P(("batch", "item")),
        P("batch", "item", None, None),
        P(("batch", "item")),
        P(("batch", "item")),
    )
    return jax.shard_map(
        on_device,
        mesh=mesh,
        in_specs=placed,
        out_specs=(
            P(("batch", "item"), None),
            P(("batch", "item")),
            P(("batch", "item"), None),
            P(),
        ),
        check_vma=False,
    )
```

```python
import functools
import math

import jax
import jax.numpy as jnp
from jax import lax
from jax.experimental import pallas as pl
from jax.experimental.pallas import tpu as pltpu
from jax.sharding import PartitionSpec as P

BF = jnp.bfloat16
F32 = jnp.float32
VM = pl.BlockSpec(memory_space=pltpu.VMEM)
ANY = pl.BlockSpec(memory_space=pl.ANY)
NN = (((1,), (0,)), ((), ()))
NT = (((1,), (1,)), ((), ()))
MIB = 1024 * 1024


def mm(a, b, dims=NN):
    return lax.dot_general(a, b, dims, preferred_element_type=F32)


def split(x):
    hi = x.astype(BF)
    return hi, (x - hi.astype(F32)).astype(BF)


def matches(rows, index):
    shape16 = (16, index.shape[1])
    index = jnp.broadcast_to(index, shape16).astype(jnp.int16)
    line = lax.broadcasted_iota(jnp.int32, shape16, 0).astype(jnp.int16)
    return [line + jnp.int16(s) == index for s in range(0, rows, 16)]


def one_hot(rows, index):
    one, zero = jnp.ones((16, index.shape[1]), BF), jnp.zeros((16, index.shape[1]), BF)
    return jnp.concatenate([jnp.where(m, one, zero) for m in matches(rows, index)], axis=0)


def signed_hot(rows, plus, minus):
    same = plus == minus
    one, zero = jnp.ones((16, plus.shape[1]), BF), jnp.zeros((16, plus.shape[1]), BF)
    up = matches(rows, jnp.where(same, -1, plus))
    down = matches(rows, jnp.where(same, -1, minus))
    return jnp.concatenate(
        [jnp.where(p, one, jnp.where(m, -one, zero)) for p, m in zip(up, down)], axis=0
    )


def lane_index(ref, first, count):
    return jnp.concatenate([ref[r : r + 1, :] for r in range(first, first + count)], axis=1)


def fold(block):
    half = block.shape[0] // 2
    return jnp.concatenate([block[:half], block[half:]], axis=1)


def widen(block):
    return jnp.concatenate([block, jnp.zeros(block.shape, F32)], axis=1)


def pair(ref, o, lines, side, cap):
    cols = slice(side * cap, (side + 1) * cap)
    a, b = take(ref, o)[lines], take(ref, o + 1)[lines]
    return jnp.concatenate([a[:, cols], b[:, cols]], axis=1)


def put(ref, o, block, w2):
    _, parts, lines, span = ref.shape
    ref[o, : parts - 1] = fold(block[:w2]).astype(BF).reshape(parts - 1, lines, span)
    ref[o, parts - 1] = widen(block[w2 : w2 + lines]).astype(BF)


def width_of(ref):
    return (ref.shape[1] - 1) * ref.shape[2]


def take(ref, o):
    _, parts, lines, span = ref.shape
    full = ref[o, : parts - 1].reshape((parts - 1) * lines, span).astype(F32)
    bias = ref[o, parts - 1].astype(F32)
    return jnp.concatenate([full, bias, jnp.zeros(bias.shape, F32)], axis=0)


def table_kernel(feat_ref, both_ref, bias_ref, out_ref):
    rows, feats = feat_ref.shape
    width = both_ref.shape[0]
    out_ref[0:width, :] = both_ref[:, feats:]
    out_ref[width : 2 * width, :] = mm(both_ref[:, :feats], feat_ref[...], NT).astype(BF)
    first = lax.broadcasted_iota(jnp.int32, (16, rows), 0) == 0
    bias = jnp.where(first, bias_ref[...].astype(F32), 0.0)
    out_ref[2 * width :, :] = bias.astype(BF)


def send_kernel(table_ref, asked_ref, out_ref):
    owners, cap = asked_ref.shape
    rows = table_ref.shape[1]
    w2 = table_ref.shape[0] - 16
    table = table_ref[...]
    for o in range(0, owners, 4):
        hot = one_hot(rows, lane_index(asked_ref, o, 4))
        got = mm(table, hot)
        for k in range(4):
            block = got[:, k * cap : (k + 1) * cap]
            put(out_ref, o + k, block, w2)


def flatten(in_ref, flat, cap):
    owners, width = in_ref.shape[0], width_of(in_ref)
    for o in range(0, owners, 2):
        cols = slice(o * cap, (o + 2) * cap)
        flat[0:width, cols] = pair(in_ref, o, slice(0, width), 0, cap).astype(BF)
        flat[width : 2 * width, cols] = pair(in_ref, o, slice(0, width), 1, cap).astype(BF)
        bias = pair(in_ref, o, slice(width, width + 8), 0, cap)
        bias = jnp.concatenate([bias, jnp.zeros(bias.shape, F32)], axis=0)
        flat[2 * width :, cols] = bias.astype(BF)


def triple_kernel(
    got_ref, user_ref, uid_ref, pos_ref, neg_ref, send_ref, ugrad_out, flat, diff, grad, ugd, picked, ugrad, sem
):
    owners, cap = got_ref.shape[0], got_ref.shape[3] // 2
    width = width_of(got_ref)
    w2 = 2 * width
    high = w2 + 16
    slots = owners * cap
    users = user_ref.shape[0]
    flatten(got_ref, flat, cap)
    user_table = jnp.transpose(user_ref[...].astype(F32)).astype(BF)
    step = 2 * pos_ref.shape[1]
    table = flat[...]
    for r in range(0, pos_ref.shape[0], 2):
        cols = slice(r // 2 * step, (r // 2 + 1) * step)
        diff[:, cols] = signed_hot(slots, lane_index(pos_ref, r, 2), lane_index(neg_ref, r, 2))
        delta = mm(table, diff[:, cols])
        mine = one_hot(users, lane_index(uid_ref, r, 2))
        picked[:, cols] = mine
        u = mm(user_table, mine)
        x = jnp.sum(u * delta[:w2], axis=0, keepdims=True) + delta[w2 : w2 + 1]
        g = -jax.nn.sigmoid(-x)
        hi, lo = split(g * u)
        first = lax.broadcasted_iota(jnp.int32, (16, step), 0) == 0
        bhi, blo = split(jnp.where(first, g, 0.0))
        grad[0:w2, cols] = hi
        grad[w2:high, cols] = bhi
        grad[high : high + w2, cols] = lo
        grad[high + w2 :, cols] = blo
        hi, lo = split(g * delta[:w2])
        ugd[0:w2, cols] = hi
        ugd[w2:, cols] = lo
    both = mm(picked[...], ugd[...], NT)
    ugrad[...] = both[:, :w2] + both[:, w2:]
    copy = pltpu.make_async_copy(ugrad, ugrad_out, sem)
    copy.start()
    both = grad[...]
    for o in range(0, owners, 8):
        out = mm(both, diff[o * cap : (o + 8) * cap, :], NT)
        out = out[:high] + out[high:]
        for k in range(8):
            block = out[:, k * cap : (k + 1) * cap]
            put(send_ref, o + k, block, w2)
    copy.wait()


def block_of(ref, o, chunks):
    _, lines, span = chunks.shape
    i, j = divmod(o, ref.shape[1] // span)
    return ref[i * lines : (i + 1) * lines, j * span : (j + 1) * span]


def term_kernel(back_ref, asked_ref, feat_ref, lat_ref, bias_ref, out_ref):
    owners, cap = asked_ref.shape
    width = width_of(back_ref)
    rows = feat_ref.shape[0]
    total = jnp.zeros((2 * width + 16, rows), F32)
    for o in range(0, owners, 8):
        parts = []
        for k in range(o, o + 8, 2):
            bias = pair(back_ref, k, slice(width, width + 8), 0, cap)
            both = [pair(back_ref, k, slice(0, width), side, cap) for side in range(2)]
            parts.append(jnp.concatenate([*both, bias, jnp.zeros(bias.shape, F32)], axis=0))
        part = jnp.concatenate(parts, axis=1).astype(BF)
        total = total + mm(part, one_hot(rows, lane_index(asked_ref, o, 8)), NT)
    lat_ref[...] = total[:width]
    bias_ref[...] = total[2 * width : 2 * width + 1]
    total = total[width : 2 * width]
    hi, lo = split(total)
    both = mm(jnp.concatenate([hi, lo], axis=0), feat_ref[...])
    term = both[:width] + both[width:]
    for o in range(owners):
        out_ref[o] = block_of(term, o, out_ref)


def sum_kernel(in_ref, out_ref, *, scale):
    total = in_ref[0].astype(F32)
    for k in range(1, in_ref.shape[0]):
        total = total + in_ref[k].astype(F32)
    out_ref[...] = jnp.broadcast_to((total * scale)[None], out_ref.shape).astype(out_ref.dtype)


def join_kernel(in_ref, lat_ref, bias_ref, out_hbm, lat_hbm, bias_hbm, out_ref, sems):
    moves = [(lat_ref, lat_hbm), (bias_ref, bias_hbm), (out_ref, out_hbm)]
    copies = [pltpu.make_async_copy(a, b, sems.at[i]) for i, (a, b) in enumerate(moves)]
    for copy in copies[:2]:
        copy.start()
    owners, lines, span = in_ref.shape
    across = out_ref.shape[1] // span
    for o in range(0, owners, 2 * across):
        i = o // across * lines
        for j in range(across):
            pair = [in_ref[o + j].astype(F32), in_ref[o + across + j].astype(F32)]
            columns = slice(j * span, (j + 1) * span)
            out_ref[i : i + 2 * lines, columns] = jnp.concatenate(pair, axis=0)
    copies[2].start()
    for copy in copies:
        copy.wait()


def call(kernel, out, *args, scratch=(), limit=8, flops=0, moved=0, **more):
    many = isinstance(out, (list, tuple))
    more.setdefault("in_specs", [VM] * len(args))
    more.setdefault("out_specs", [VM] * len(out) if many else VM)
    return pl.pallas_call(
        kernel,
        out_shape=out,
        scratch_shapes=list(scratch),
        compiler_params=pltpu.CompilerParams(vmem_limit_bytes=limit * MIB),
        cost_estimate=pl.CostEstimate(flops=flops, bytes_accessed=moved, transcendentals=0),
        **more,
    )(*args)


def shape(dims, dtype):
    return jax.ShapeDtypeStruct(dims, dtype)


def exchange(x, axis):
    return lax.all_to_all(x, axis, split_axis=0, concat_axis=0, tiled=True)


def on_device(
    item_feat,
    item_latent,
    item_bias,
    projection,
    user_factors,
    user_ids,
    requests,
    pos_slot,
    neg_slot,
):
    owners = lax.axis_size("item")
    groups = lax.axis_size("batch")
    rows, feats = item_feat.shape
    width = item_latent.shape[1]
    users = user_factors.shape[0]
    cap = requests.shape[-1]
    slots = owners * cap
    triples = pos_slot.shape[0]
    w2 = 2 * width
    high = w2 + 16
    rows128 = triples // 128

    asked = exchange(requests.reshape(owners, cap), "item")
    pos = pos_slot.reshape(rows128, 128)
    neg = neg_slot.reshape(rows128, 128)
    uid = user_ids.reshape(rows128, 128)
    table = call(
        table_kernel,
        shape((high, rows), BF),
        item_feat,
        jnp.concatenate([projection.T, item_latent.T], axis=1),
        item_bias.reshape(1, rows),
        flops=2 * rows * feats * width,
        moved=2 * rows * (feats + high),
    )
    lines = 4
    message = shape((owners, width // lines + 1, lines, 2 * cap), BF)
    sent = call(send_kernel, message, table, asked, flops=2 * rows * slots * high)
    got = exchange(sent, "item")
    back, user_grad = call(
        triple_kernel,
        [message, shape((users, w2), F32)],
        got,
        user_factors,
        uid,
        pos,
        neg,
        scratch=[
            pltpu.VMEM((high, slots), BF),
            pltpu.VMEM((slots, triples), BF),
            pltpu.VMEM((2 * high, triples), BF),
            pltpu.VMEM((2 * w2, triples), BF),
            pltpu.VMEM((users, triples), BF),
            pltpu.VMEM((users, w2), F32),
            pltpu.SemaphoreType.DMA,
        ],
        out_specs=[VM, ANY],
        limit=24,
        flops=6 * slots * triples * high,
    )
    back = exchange(back, "item")
    chunk = (lines, width * feats // owners // lines)
    lat_grad, bias_grad, term = call(
        term_kernel,
        [shape((width, rows), F32), shape((1, rows), F32), shape((owners, *chunk), F32)],
        back,
        asked,
        item_feat,
        flops=2 * rows * slots * high,
    )
    parts = exchange(term, "item")
    total = triples * groups * owners
    group_sum = call(
        functools.partial(sum_kernel, scale=1.0), shape((groups, *chunk), BF), parts
    )
    parts = exchange(group_sum, "batch")
    whole = call(
        functools.partial(sum_kernel, scale=1.0 / math.sqrt(total)),
        shape((owners, *chunk), BF),
        parts,
    )
    parts = exchange(whole, "item")
    projection_grad, lat_grad, bias_grad = call(
        join_kernel,
        [shape((width, feats), F32), shape((width, rows), F32), shape((1, rows), F32)],
        parts,
        lat_grad,
        bias_grad,
        out_specs=[ANY] * 3,
        scratch=[pltpu.VMEM((width, feats), F32), pltpu.SemaphoreType.DMA((3,))],
    )
    return (lat_grad.T, bias_grad.reshape(rows), user_grad, projection_grad.T)


def solution(mesh):
    placed = (
        P(("batch", "item"), None),
        P(("batch", "item"), None),
        P(("batch", "item")),
        P(),
        P(("batch", "item"), None),
        P(("batch", "item")),
        P("batch", "item", None, None),
        P(("batch", "item")),
        P(("batch", "item")),
    )
    return jax.shard_map(
        on_device,
        mesh=mesh,
        in_specs=placed,
        out_specs=(
            P(("batch", "item"), None),
            P(("batch", "item")),
            P(("batch", "item"), None),
            P(),
        ),
        check_vma=False,
    )
```

```python
import functools
import math

import jax
import jax.numpy as jnp
from jax import lax
from jax.experimental import pallas as pl
from jax.experimental.pallas import tpu as pltpu
from jax.sharding import PartitionSpec as P

BF = jnp.bfloat16
F32 = jnp.float32
VM = pl.BlockSpec(memory_space=pltpu.VMEM)
ANY = pl.BlockSpec(memory_space=pl.ANY)
NN = (((1,), (0,)), ((), ()))
NT = (((1,), (1,)), ((), ()))
MIB = 1024 * 1024


def mm(a, b, dims=NN):
    return lax.dot_general(a, b, dims, preferred_element_type=F32)


def split(x):
    hi = x.astype(BF)
    return hi, (x - hi.astype(F32)).astype(BF)


def matches(rows, index):
    shape16 = (16, index.shape[1])
    index = jnp.broadcast_to(index, shape16).astype(jnp.int16)
    line = lax.broadcasted_iota(jnp.int32, shape16, 0).astype(jnp.int16)
    return [line + jnp.int16(s) == index for s in range(0, rows, 16)]


def one_hot(rows, index):
    one, zero = jnp.ones((16, index.shape[1]), BF), jnp.zeros((16, index.shape[1]), BF)
    return jnp.concatenate([jnp.where(m, one, zero) for m in matches(rows, index)], axis=0)


def signed_hot(rows, plus, minus):
    same = plus == minus
    one, zero = jnp.ones((16, plus.shape[1]), BF), jnp.zeros((16, plus.shape[1]), BF)
    up = matches(rows, jnp.where(same, -1, plus))
    down = matches(rows, jnp.where(same, -1, minus))
    return jnp.concatenate(
        [jnp.where(p, one, jnp.where(m, -one, zero)) for p, m in zip(up, down)], axis=0
    )


def lane_index(ref, first, count):
    return jnp.concatenate([ref[r : r + 1, :] for r in range(first, first + count)], axis=1)


def fold(block):
    half = block.shape[0] // 2
    return jnp.concatenate([block[:half], block[half:]], axis=1)


def widen(block):
    return jnp.concatenate([block, jnp.zeros(block.shape, F32)], axis=1)


def pair(ref, o, lines, side, cap):
    cols = slice(side * cap, (side + 1) * cap)
    a, b = take(ref, o)[lines], take(ref, o + 1)[lines]
    return jnp.concatenate([a[:, cols], b[:, cols]], axis=1)


def put(ref, o, block, w2):
    _, parts, lines, span = ref.shape
    ref[o, : parts - 1] = fold(block[:w2]).astype(BF).reshape(parts - 1, lines, span)
    ref[o, parts - 1] = widen(block[w2 : w2 + lines]).astype(BF)


def width_of(ref):
    return (ref.shape[1] - 1) * ref.shape[2]


def take(ref, o):
    _, parts, lines, span = ref.shape
    full = ref[o, : parts - 1].reshape((parts - 1) * lines, span).astype(F32)
    bias = ref[o, parts - 1].astype(F32)
    return jnp.concatenate([full, bias, jnp.zeros(bias.shape, F32)], axis=0)


def table_kernel(feat_ref, both_ref, bias_ref, out_ref):
    rows, feats = feat_ref.shape
    width = both_ref.shape[0]
    out_ref[0:width, :] = both_ref[:, feats:]
    out_ref[width : 2 * width, :] = mm(both_ref[:, :feats], feat_ref[...], NT).astype(BF)
    first = lax.broadcasted_iota(jnp.int32, (16, rows), 0) == 0
    bias = jnp.where(first, bias_ref[...].astype(F32), 0.0)
    out_ref[2 * width :, :] = bias.astype(BF)


def send_kernel(table_ref, asked_ref, out_ref):
    owners, cap = asked_ref.shape
    rows = table_ref.shape[1]
    w2 = table_ref.shape[0] - 16
    table = table_ref[...]
    for o in range(0, owners, 4):
        hot = one_hot(rows, lane_index(asked_ref, o, 4))
        got = mm(table, hot)
        for k in range(4):
            block = got[:, k * cap : (k + 1) * cap]
            put(out_ref, o + k, block, w2)


def flatten(in_ref, flat, cap):
    owners, width = in_ref.shape[0], width_of(in_ref)
    for o in range(0, owners, 2):
        cols = slice(o * cap, (o + 2) * cap)
        flat[0:width, cols] = pair(in_ref, o, slice(0, width), 0, cap).astype(BF)
        flat[width : 2 * width, cols] = pair(in_ref, o, slice(0, width), 1, cap).astype(BF)
        bias = pair(in_ref, o, slice(width, width + 8), 0, cap)
        bias = jnp.concatenate([bias, jnp.zeros(bias.shape, F32)], axis=0)
        flat[2 * width :, cols] = bias.astype(BF)


def triple_kernel(
    got_ref, user_ref, uid_ref, pos_ref, neg_ref, send_ref, ugrad_out, flat, diff, grad, ugd, picked, ugrad, sem
):
    owners, cap = got_ref.shape[0], got_ref.shape[3] // 2
    width = width_of(got_ref)
    w2 = 2 * width
    high = w2 + 16
    slots = owners * cap
    users = user_ref.shape[0]
    flatten(got_ref, flat, cap)
    user_table = jnp.transpose(user_ref[...].astype(F32)).astype(BF)
    step = 2 * pos_ref.shape[1]
    table = flat[...]
    for r in range(0, pos_ref.shape[0], 2):
        cols = slice(r // 2 * step, (r // 2 + 1) * step)
        diff[:, cols] = signed_hot(slots, lane_index(pos_ref, r, 2), lane_index(neg_ref, r, 2))
        delta = mm(table, diff[:, cols])
        mine = one_hot(users, lane_index(uid_ref, r, 2))
        picked[:, cols] = mine
        u = mm(user_table, mine)
        x = jnp.sum(u * delta[:w2], axis=0, keepdims=True) + delta[w2 : w2 + 1]
        g = -jax.nn.sigmoid(-x)
        hi, lo = split(g * u)
        first = lax.broadcasted_iota(jnp.int32, (16, step), 0) == 0
        bhi, blo = split(jnp.where(first, g, 0.0))
        grad[0:w2, cols] = hi
        grad[w2:high, cols] = bhi
        grad[high : high + w2, cols] = lo
        grad[high + w2 :, cols] = blo
        hi, lo = split(g * delta[:w2])
        ugd[0:w2, cols] = hi
        ugd[w2:, cols] = lo
    both = mm(picked[...], ugd[...], NT)
    ugrad[...] = both[:, :w2] + both[:, w2:]
    copy = pltpu.make_async_copy(ugrad, ugrad_out, sem)
    copy.start()
    both = grad[...]
    for o in range(0, owners, 16):
        out = mm(both, diff[o * cap : (o + 16) * cap, :], NT)
        out = out[:high] + out[high:]
        for k in range(16):
            block = out[:, k * cap : (k + 1) * cap]
            put(send_ref, o + k, block, w2)
    copy.wait()


def block_of(ref, o, chunks):
    _, lines, span = chunks.shape
    i, j = divmod(o, ref.shape[1] // span)
    return ref[i * lines : (i + 1) * lines, j * span : (j + 1) * span]


def term_kernel(back_ref, asked_ref, feat_ref, lat_ref, bias_ref, out_ref):
    owners, cap = asked_ref.shape
    width = width_of(back_ref)
    rows = feat_ref.shape[0]
    total = jnp.zeros((2 * width + 16, rows), F32)
    for o in range(0, owners, 8):
        parts = []
        for k in range(o, o + 8, 2):
            bias = pair(back_ref, k, slice(width, width + 8), 0, cap)
            both = [pair(back_ref, k, slice(0, width), side, cap) for side in range(2)]
            parts.append(jnp.concatenate([*both, bias, jnp.zeros(bias.shape, F32)], axis=0))
        part = jnp.concatenate(parts, axis=1).astype(BF)
        total = total + mm(part, one_hot(rows, lane_index(asked_ref, o, 8)), NT)
    lat_ref[...] = total[:width]
    bias_ref[...] = total[2 * width : 2 * width + 1]
    total = total[width : 2 * width]
    hi, lo = split(total)
    both = mm(jnp.concatenate([hi, lo], axis=0), feat_ref[...])
    term = both[:width] + both[width:]
    for o in range(owners):
        out_ref[o] = block_of(term, o, out_ref)


def sum_kernel(in_ref, out_ref, *, scale):
    total = in_ref[0].astype(F32)
    for k in range(1, in_ref.shape[0]):
        total = total + in_ref[k].astype(F32)
    out_ref[...] = jnp.broadcast_to((total * scale)[None], out_ref.shape).astype(out_ref.dtype)


def join_kernel(in_ref, lat_ref, bias_ref, out_hbm, lat_hbm, bias_hbm, out_ref, sems):
    moves = [(lat_ref, lat_hbm), (bias_ref, bias_hbm), (out_ref, out_hbm)]
    copies = [pltpu.make_async_copy(a, b, sems.at[i]) for i, (a, b) in enumerate(moves)]
    for copy in copies[:2]:
        copy.start()
    owners, lines, span = in_ref.shape
    across = out_ref.shape[1] // span
    for o in range(0, owners, 2 * across):
        i = o // across * lines
        for j in range(across):
            pair = [in_ref[o + j].astype(F32), in_ref[o + across + j].astype(F32)]
            columns = slice(j * span, (j + 1) * span)
            out_ref[i : i + 2 * lines, columns] = jnp.concatenate(pair, axis=0)
    copies[2].start()
    for copy in copies:
        copy.wait()


def call(kernel, out, *args, scratch=(), limit=8, flops=0, moved=0, **more):
    many = isinstance(out, (list, tuple))
    more.setdefault("in_specs", [VM] * len(args))
    more.setdefault("out_specs", [VM] * len(out) if many else VM)
    return pl.pallas_call(
        kernel,
        out_shape=out,
        scratch_shapes=list(scratch),
        compiler_params=pltpu.CompilerParams(vmem_limit_bytes=limit * MIB),
        cost_estimate=pl.CostEstimate(flops=flops, bytes_accessed=moved, transcendentals=0),
        **more,
    )(*args)


def shape(dims, dtype):
    return jax.ShapeDtypeStruct(dims, dtype)


def exchange(x, axis):
    return lax.all_to_all(x, axis, split_axis=0, concat_axis=0, tiled=True)


def on_device(
    item_feat,
    item_latent,
    item_bias,
    projection,
    user_factors,
    user_ids,
    requests,
    pos_slot,
    neg_slot,
):
    owners = lax.axis_size("item")
    groups = lax.axis_size("batch")
    rows, feats = item_feat.shape
    width = item_latent.shape[1]
    users = user_factors.shape[0]
    cap = requests.shape[-1]
    slots = owners * cap
    triples = pos_slot.shape[0]
    w2 = 2 * width
    high = w2 + 16
    rows128 = triples // 128

    asked = exchange(requests.reshape(owners, cap), "item")
    pos = pos_slot.reshape(rows128, 128)
    neg = neg_slot.reshape(rows128, 128)
    uid = user_ids.reshape(rows128, 128)
    table = call(
        table_kernel,
        shape((high, rows), BF),
        item_feat,
        jnp.concatenate([projection.T, item_latent.T], axis=1),
        item_bias.reshape(1, rows),
        flops=2 * rows * feats * width,
        moved=2 * rows * (feats + high),
    )
    lines = 4
    message = shape((owners, width // lines + 1, lines, 2 * cap), BF)
    sent = call(send_kernel, message, table, asked, flops=2 * rows * slots * high)
    got = exchange(sent, "item")
    back, user_grad = call(
        triple_kernel,
        [message, shape((users, w2), F32)],
        got,
        user_factors,
        uid,
        pos,
        neg,
        scratch=[
            pltpu.VMEM((high, slots), BF),
            pltpu.VMEM((slots, triples), BF),
            pltpu.VMEM((2 * high, triples), BF),
            pltpu.VMEM((2 * w2, triples), BF),
            pltpu.VMEM((users, triples), BF),
            pltpu.VMEM((users, w2), F32),
            pltpu.SemaphoreType.DMA,
        ],
        out_specs=[VM, ANY],
        limit=24,
        flops=6 * slots * triples * high,
    )
    back = exchange(back, "item")
    chunk = (lines, width * feats // owners // lines)
    lat_grad, bias_grad, term = call(
        term_kernel,
        [shape((width, rows), F32), shape((1, rows), F32), shape((owners, *chunk), F32)],
        back,
        asked,
        item_feat,
        flops=2 * rows * slots * high,
    )
    parts = exchange(term, "item")
    total = triples * groups * owners
    group_sum = call(
        functools.partial(sum_kernel, scale=1.0), shape((groups, *chunk), BF), parts
    )
    parts = exchange(group_sum, "batch")
    whole = call(
        functools.partial(sum_kernel, scale=1.0 / math.sqrt(total)),
        shape((owners, *chunk), BF),
        parts,
    )
    parts = exchange(whole, "item")
    projection_grad, lat_grad, bias_grad = call(
        join_kernel,
        [shape((width, feats), F32), shape((width, rows), F32), shape((1, rows), F32)],
        parts,
        lat_grad,
        bias_grad,
        out_specs=[ANY] * 3,
        scratch=[pltpu.VMEM((width, feats), F32), pltpu.SemaphoreType.DMA((3,))],
    )
    return (lat_grad.T, bias_grad.reshape(rows), user_grad, projection_grad.T)


def solution(mesh):
    placed = (
        P(("batch", "item"), None),
        P(("batch", "item"), None),
        P(("batch", "item")),
        P(),
        P(("batch", "item"), None),
        P(("batch", "item")),
        P("batch", "item", None, None),
        P(("batch", "item")),
        P(("batch", "item")),
    )
    return jax.shard_map(
        on_device,
        mesh=mesh,
        in_specs=placed,
        out_specs=(
            P(("batch", "item"), None),
            P(("batch", "item")),
            P(("batch", "item"), None),
            P(),
        ),
        check_vma=False,
    )
```
